32 devices in a mesh: seq: 16 (over z, y, x), head: 2 (over core).
Axes of the slice: x: 2, y: 2, z: 4, core: 2. Of those that a mesh axis runs over, the one named last changes fastest.
Arguments:
- hidden: bfloat16 [2048, 2048], P('seq'), may hold values from -6 to 6
- queries: bfloat16 [2048, 3072], P('seq', 'head'), may hold values from -90 to 90
- req_len: int32 [2], replicated, may hold values from 1 to 1920, 2048 in all
- req_offset: int32 [2], replicated, may hold values from 0 to 4095
- expert_ids: int32 [2048, 6], P('seq'), may hold values from 0 to 15, all different within a row; in each aligned block of 128 rows (0 to 127, 128 to 255, ...) at most 64 rows name the same one
- decode_slot: int32 [128], replicated, may hold values from 0 to 127, as said below
- attn_gain: float32 [2048], replicated, may hold values from 0.25 to 1.75
- kv_down: bfloat16 [2048, 576], replicated, may hold values from -0.125 to 0.125
- kv_gain: float32 [512], replicated, may hold values from 0.25 to 1.75
- key_up: bfloat16 [16, 128, 512], P('head'), may hold values from -0.5 to 0.5
- value_up: bfloat16 [16, 512, 128], P('head'), may hold values from -0.25 to 0.25
- out_proj: bfloat16 [2048, 2048], P('head'), may hold values from -0.5 to 0.5
- ffn_gain: float32 [2048], replicated, may hold values from 0.25 to 1.75
- router: float32 [2048, 16], replicated, may hold values from -0.125 to 0.125
- expert_gate_up: bfloat16 [16, 2, 2048, 1408], P('seq', None, None, 'head'), may hold values from -0.125 to 0.125
- expert_down: bfloat16 [16, 1408, 2048], P('seq', 'head'), may hold values from -0.15625 to 0.15625
Outputs:
- output: bfloat16 [2048, 2048], P('seq', 'head')
- decode_latent: bfloat16 [128, 16, 512], P(('seq', 'head'))
- decode_rope: bfloat16 [128, 1024], P(('seq', 'head'))
The draws below stay inside these ranges and needn't reach their ends.
Inputs may be any that keep to these rules, and one draw needn't show every extreme that they name: `req_len`: the lengths sum to 2048. `expert_ids`: the 128 rows of one index of seq name one expert at most 64 times in all. `decode_slot`: all entries differ; slot g belongs to device g // 4 in the order seq then head, and all 4 slots of some device are named.
All inputs are finite; a program needn't handle non-finite values.
Results may differ from the reference program's by a relative error of at most 0.02.
Values may be sent and summed in bfloat16 or wider, within the bound.
A program may use at most 128 MiB of HBM per device.

```python
import math
import jax
import jax.numpy as jnp
import numpy as np
from jax import lax

D = 2048
N_HEADS = 16
NOPE = 128
ROPE = 64
V_HEAD = 128
KV_RANK = 512
FF = 1408
TOP = 6
TOK_DEV = 128
BLOCK = 16
DEC_SLOTS = 4
EXPERTS = 16
TOKENS = 2048
NREQ = 2
MAXLEN = 1920
NBLK = 128
TOTAL_SLOTS = 128
CAP = 64
N_SEQ = 16
N_HEAD = 2


def draw_queries(key, part):
    shape_all = (TOKENS, N_HEADS * (NOPE + ROPE))
    values = jax.random.normal(key, shape_all, jnp.float32)
    return jnp.clip(values, -90.0, 90.0).astype(jnp.bfloat16)


def draw_decode_slot(key, part):
    first_key, second_key, third_key = jax.random.split(key, 3)
    owners = TOTAL_SLOTS // DEC_SLOTS
    full_owner = jax.random.randint(first_key, (), 0, owners)
    slot_ids = jnp.arange(TOTAL_SLOTS, dtype=jnp.int32)
    ranking = jax.random.randint(second_key, (TOTAL_SLOTS,), 0, 65536)
    ranking = jnp.where(slot_ids // DEC_SLOTS == full_owner, 65536, ranking)
    ranking = ranking * TOTAL_SLOTS + slot_ids
    chosen = lax.top_k(ranking, NBLK)[1].astype(jnp.int32)
    return jax.random.permutation(third_key, chosen).astype(jnp.int32)


def level_of(stream_key, extent, cuts, smallest, largest):
    def one(dim, parts):
        heights = jax.random.uniform(jax.random.fold_in(jax.random.fold_in(stream_key, 6), dim), (parts,), jnp.float32, smallest / len(cuts), largest / len(cuts))
        return jnp.repeat(jnp.exp(heights), extent[dim] // parts).reshape((-1,) + (1,) * (len(extent) - dim - 1))

    factor_of = one(*cuts[0])
    for cut in cuts[1:]:
        factor_of = factor_of * one(*cut)
    return factor_of


def length_profile(amount, total, limit, slope):
    loads = [(1 << 20) // math.isqrt(grade ** slope) + 1 for grade in range(2, amount + 1)]
    rest, given = total - limit - (amount - 1), [1] * (amount - 1)
    while rest > 0:
        free = [i for i in range(amount - 1) if given[i] < limit]
        whole, left = sum([loads[i] for i in free]), rest
        for i in free:
            addition = min(limit - given[i], max(1, left * loads[i] // whole), rest)
            given[i] = given[i] + addition
            rest = rest - addition
    return np.array([limit] + given)


def uneven(stream_key, number_of, total, limit, skew):
    if number_of == 2:
        one = jax.random.randint(stream_key, (), max(1, total - limit), min(limit, total - 1) + 1)
        return jnp.stack([one, total - one])
    sizes = jnp.asarray(length_profile(number_of, total, limit, skew), jnp.int32)
    couples = (number_of - 1) // 2
    giver, sink = sizes[1:1 + 2 * couples:2], sizes[2:2 + 2 * couples:2]
    room = jnp.minimum(giver - 1, limit - sink)
    shifted = jax.random.randint(jax.random.fold_in(stream_key, 1), (couples,), 0, 1 << 20) % (room + 1)
    sizes = sizes.at[1:1 + 2 * couples:2].set(giver - shifted).at[2:2 + 2 * couples:2].set(sink + shifted)
    return sizes[jax.random.permutation(jax.random.fold_in(stream_key, 2), number_of)]


def deal_out(stream_key, own, number, rows, number_of, top, limit, skew):
    order = jax.random.permutation(stream_key, number_of)
    crowded, common = load_shares(number_of, rows * top, limit, skew, True), load_shares(number_of, rows * top, limit, skew, False)
    places = jnp.arange(number_of)

    def named(sizes, turn):
        used = int((sizes > 0).sum())
        fixed = max(1, used // 4)
        passed = fixed + (places - fixed + turn * (used - fixed)) % max(1, number_of - fixed)
        return jnp.zeros((number_of,), jnp.int32).at[order[jnp.where(places < fixed, places, passed)]].set(jnp.asarray(sizes, jnp.int32))

    sizes = jnp.where(number % 4 == 0, named(crowded, number // 4), named(common, number - number // 4 - 1))
    mixed = jax.random.permutation(jax.random.fold_in(own, 3), number_of)
    donor, sink = mixed[0:number_of // 2 * 2:2], mixed[1:number_of // 2 * 2:2]
    margin = jnp.minimum(sizes[donor] - 1, limit - sizes[sink]) // 2
    margin = jnp.where((donor == order[0]) | (sink == order[0]) | (sizes[sink] == 0), 0, jnp.maximum(margin, 0))
    passed = jax.random.randint(jax.random.fold_in(own, 4), (number_of // 2,), 0, 1 << 20) % (margin + 1)
    sizes = sizes.at[donor].add(-passed).at[sink].add(passed)
    members = jnp.searchsorted(jnp.cumsum(sizes), jnp.arange(rows * top), side="right").astype(jnp.int32)
    table = members.reshape(top, rows).T
    table = table[jax.random.permutation(jax.random.fold_in(own, 1), rows)]
    turn = jax.random.randint(jax.random.fold_in(own, 2), (rows, 1), 0, top)
    return jnp.take_along_axis(table, (jnp.arange(top)[None, :] + turn) % top, axis=1)


def load_shares(number_of, total, limit, slope, full):
    weights = [(1 << 20) // math.isqrt(grade ** slope) + 1 for grade in range(1, number_of + 1)]
    largest = limit if full else min(limit, max(-(-total // number_of), total * weights[0] // sum(weights)))
    least = 1 if total - largest >= number_of - 1 else 0
    given, spare = [largest] + [least] * (number_of - 1), total - largest - least * (number_of - 1)
    while spare > 0:
        candidates = [i for i in range(1, number_of) if given[i] < largest] or [i for i in range(1, number_of) if given[i] < limit]
        whole, budget = sum([weights[i] for i in candidates]), spare
        for i in candidates:
            more = min(limit - given[i], max(1, budget * weights[i] // whole), spare)
            given[i] = given[i] + more
            spare = spare - more
    return np.array(given)


def scatter_about(own_key, shape, spread, reach, cuts=(), kind=jnp.bfloat16):
    loudness = level_of(own_key, shape, cuts, -0.22, 0.18) if cuts else 1.0
    values = jax.random.normal(own_key, shape, jnp.float32) * spread * loudness
    return jnp.minimum(jnp.maximum(values, -reach), reach).astype(kind)


def setup_inputs(seed: int = 0) -> dict:
    keys = jax.random.split(jax.random.key(seed), 17)
    hidden = scatter_about(keys[0], (TOKENS, D), 1.0, 6.0, ((0, 16),))
    queries = draw_queries(jax.random.fold_in(keys[16], 71), 0)
    req_len = uneven(keys[2], NREQ, TOKENS, MAXLEN, 2).astype(jnp.int32)
    req_offset = jax.random.randint(keys[3], (NREQ,), 0, 4096).astype(jnp.int32)
    expert_ids_keys = jax.random.split(jax.random.fold_in(keys[4], 1), TOKENS // TOK_DEV)
    expert_ids_turns = jax.random.permutation(jax.random.fold_in(keys[4], 3), TOKENS // TOK_DEV)
    expert_ids = jax.vmap(lambda own, number: deal_out(jax.random.fold_in(keys[4], 2), own, number, TOK_DEV, EXPERTS, TOP, CAP, 2))(expert_ids_keys, expert_ids_turns).reshape((TOKENS, TOP))
    decode_slot = draw_decode_slot(jax.random.fold_in(keys[16], 71), 0)
    attn_gain = jnp.clip(1.0 + 0.15 * jax.random.normal(keys[6], (D,), jnp.float32), 0.25, 1.75)
    kv_down = scatter_about(keys[7], (D, KV_RANK + ROPE), D ** -0.5, 0.125)
    kv_gain = jnp.clip(1.0 + 0.15 * jax.random.normal(keys[8], (KV_RANK,), jnp.float32), 0.25, 1.75)
    key_up = scatter_about(keys[9], (N_HEADS, NOPE, KV_RANK), NOPE ** -0.5, 0.5, ((0, 2),))
    value_up = scatter_about(keys[10], (N_HEADS, KV_RANK, V_HEAD), KV_RANK ** -0.5, 0.25, ((0, 2),))
    out_proj = scatter_about(keys[11], (N_HEADS * V_HEAD, D), (N_HEADS * V_HEAD // 16) ** -0.5, 0.5, ((0, 2),))
    ffn_gain = jnp.clip(1.0 + 0.15 * jax.random.normal(keys[12], (D,), jnp.float32), 0.25, 1.75)
    router = scatter_about(keys[13], (D, EXPERTS), D ** -0.5, 0.125, (), jnp.float32)
    expert_gate_up = scatter_about(keys[14], (EXPERTS, 2, D, FF), D ** -0.5, 0.125, ((0, 16), (3, 2)))
    expert_down = scatter_about(keys[15], (EXPERTS, FF, D), FF ** -0.5, 0.15625, ((0, 16), (1, 2)))
    return dict(hidden=hidden, queries=queries, req_len=req_len, req_offset=req_offset, expert_ids=expert_ids, decode_slot=decode_slot, attn_gain=attn_gain, kv_down=kv_down, kv_gain=kv_gain, key_up=key_up, value_up=value_up, out_proj=out_proj, ffn_gain=ffn_gain, router=router, expert_gate_up=expert_gate_up, expert_down=expert_down)


ROPE_BASE = 50000.0
ROUTE_SCALE = 2.446
EPSILON = 1e-06
MASKED = -1e+30

def rms_rows(values, scale_gain):
    values = values.astype(jnp.float32)
    inverse = lax.rsqrt(lax.optimization_barrier(jnp.mean(values * values, axis=-1, keepdims=True)) + EPSILON)
    return values * inverse * scale_gain

def angles(position, rope_width):
    half_width = rope_width // 2
    freq_steps = jnp.arange(half_width).astype(jnp.float32) * (2.0 / rope_width)
    frequency = jnp.exp(-math.log(ROPE_BASE) * freq_steps)
    return position.astype(jnp.float32)[:, None] * frequency[None, :]

def rotate(values, rot_angle):
    half_width = values.shape[-1] // 2
    first_half = values[..., :half_width].astype(jnp.float32)
    second_half = values[..., half_width:].astype(jnp.float32)
    cosine = jnp.cos(rot_angle)
    sine_part = jnp.sin(rot_angle)
    return jnp.concatenate([first_half * cosine - second_half * sine_part, first_half * sine_part + second_half * cosine], axis=-1)

def request_of(req_len, token_index):
    req_ends = jnp.cumsum(req_len).astype(jnp.int32)
    return lax.optimization_barrier(jnp.sum((token_index[:, None] >= req_ends[None, :]).astype(jnp.int32), axis=1)).astype(jnp.int32)

def position_of(req_len, req_offset, token_index):
    request = request_of(req_len, token_index)
    req_ends = jnp.cumsum(req_len).astype(jnp.int32)
    starts = req_ends - req_len
    member = request[:, None] == jnp.arange(req_len.shape[0]).astype(jnp.int32)[None, :]
    start_at = lax.optimization_barrier(jnp.sum(jnp.where(member, starts[None, :], 0), axis=1))
    offset = lax.optimization_barrier(jnp.sum(jnp.where(member, req_offset[None, :], 0), axis=1))
    return (offset + token_index - start_at).astype(jnp.int32)

def reference(hidden, queries, req_len, req_offset, expert_ids, decode_slot, attn_gain, kv_down, kv_gain, key_up, value_up, out_proj, ffn_gain, router, expert_gate_up, expert_down):
    normed = rms_rows(hidden, attn_gain).astype(jnp.bfloat16)
    kv_full = jnp.dot(normed, kv_down, preferred_element_type=jnp.float32)
    latent = rms_rows(kv_full[:, :KV_RANK], kv_gain).astype(jnp.bfloat16)
    token_index = jnp.arange(TOKENS).astype(jnp.int32)
    request = request_of(req_len, token_index)
    token_turn = angles(position_of(req_len, req_offset, token_index), ROPE)
    key_rope = rotate(kv_full[:, KV_RANK:], token_turn).astype(jnp.bfloat16)
    head_view = queries.reshape(TOKENS, N_HEADS, NOPE + ROPE)
    query_rope = rotate(head_view[:, :, NOPE:], token_turn[:, None, :]).astype(jnp.bfloat16)
    query_latent = jnp.einsum('thn,hnc->thc', head_view[:, :, :NOPE].astype(jnp.float32), key_up.astype(jnp.float32)).astype(jnp.bfloat16)
    latent_wide = latent.astype(jnp.float32)
    rope_wide = key_rope.astype(jnp.float32)
    value_wide = value_up.astype(jnp.float32)
    score_scale = 1.0 / math.sqrt(NOPE + ROPE)
    block_rows = 512 if TOKENS % 512 == 0 else TOKENS

    def attend(block_no):
        first_row = block_no * block_rows
        q_latent = lax.dynamic_slice_in_dim(query_latent, first_row, block_rows, 0).astype(jnp.float32)
        q_rope = lax.dynamic_slice_in_dim(query_rope, first_row, block_rows, 0).astype(jnp.float32)
        q_index = first_row + jnp.arange(block_rows).astype(jnp.int32)
        q_request = lax.dynamic_slice_in_dim(request, first_row, block_rows, 0)
        scores = (jnp.einsum('thc,sc->ths', q_latent, latent_wide) + jnp.einsum('thr,sr->ths', q_rope, rope_wide)) * score_scale
        allowed = (token_index[None, :] <= q_index[:, None]) & (request[None, :] == q_request[:, None])
        allowed = allowed[:, None, :]
        scores = jnp.where(allowed, scores, MASKED)
        row_peak = lax.optimization_barrier(jnp.max(scores, axis=2, keepdims=True))
        exp_terms = jnp.where(allowed, jnp.exp(scores - row_peak), 0.0)
        weights = lax.optimization_barrier(exp_terms.astype(jnp.bfloat16)).astype(jnp.float32)
        attended = (jnp.einsum('ths,sc->thc', weights, latent_wide) / lax.optimization_barrier(jnp.sum(exp_terms, axis=2, keepdims=True))).astype(jnp.bfloat16)
        head_out = jnp.einsum('thc,hcv->thv', attended.astype(jnp.float32), value_wide).astype(jnp.bfloat16)
        attn_out = jnp.dot(head_out.reshape(block_rows, N_HEADS * V_HEAD), out_proj, preferred_element_type=jnp.float32)
        return lax.dynamic_slice_in_dim(hidden, first_row, block_rows, 0).astype(jnp.float32) + attn_out
    mixed_rows = lax.map(attend, jnp.arange(TOKENS // block_rows)).reshape(TOKENS, D)
    moe_in = rms_rows(mixed_rows, ffn_gain).astype(jnp.bfloat16)
    gate_score = jax.nn.sigmoid(jnp.dot(moe_in.astype(jnp.float32), router, precision=lax.Precision.HIGHEST))
    chosen = jnp.take_along_axis(gate_score, expert_ids, axis=1)
    gate_weight = ROUTE_SCALE * chosen / lax.optimization_barrier(jnp.sum(chosen, axis=1, keepdims=True))
    rows_most = N_SEQ * CAP
    quarter_units = FF // N_HEAD

    def expert_step(moe_sum, expert):
        hit_mask = expert_ids == expert
        routed = jnp.any(hit_mask, axis=1)
        weight = lax.optimization_barrier(jnp.sum(jnp.where(hit_mask, gate_weight, 0.0), axis=1))
        picked = jnp.nonzero(routed, size=rows_most, fill_value=0)[0]
        is_valid = jnp.arange(rows_most) < jnp.sum(routed.astype(jnp.int32))
        row_data = moe_in[picked]
        gate_up = expert_gate_up[expert]
        gate_part = jnp.dot(row_data, gate_up[0], preferred_element_type=jnp.float32)
        up_part = jnp.dot(row_data, gate_up[1], preferred_element_type=jnp.float32)
        activated = (jax.nn.silu(gate_part) * up_part).astype(jnp.bfloat16)
        quarters = activated.reshape(rows_most, N_HEAD, quarter_units).astype(jnp.float32)
        down_quarters = expert_down[expert].reshape(N_HEAD, quarter_units, D).astype(jnp.float32)
        part_out = jnp.einsum('rqf,qfd->rqd', quarters, down_quarters).astype(jnp.bfloat16)
        summed = lax.optimization_barrier(jnp.sum(part_out.astype(jnp.float32), axis=1))
        contribution = jnp.where(is_valid[:, None], weight[picked][:, None] * summed, 0.0)
        return (moe_sum.at[picked].add(contribution), None)
    moe_total, _ = lax.scan(expert_step, jnp.zeros((TOKENS, D), jnp.float32), jnp.arange(EXPERTS).astype(jnp.int32))
    output = (mixed_rows + moe_total).astype(jnp.bfloat16)
    decode_latent = jnp.zeros((TOTAL_SLOTS, BLOCK, KV_RANK), jnp.bfloat16).at[decode_slot].set(latent.reshape(NBLK, BLOCK, KV_RANK))
    decode_rope = jnp.zeros((TOTAL_SLOTS, BLOCK * ROPE), jnp.bfloat16).at[decode_slot].set(key_rope.reshape(NBLK, BLOCK * ROPE))
    return (output, decode_latent, decode_rope)
```

```python
import functools
import math

import jax
import jax.numpy as jnp
from jax import lax
from jax.experimental import pallas as pl
from jax.experimental.pallas import tpu as pltpu
from jax.sharding import PartitionSpec as P

D = 2048
NOPE = 128
ROPE = 64
V_HEAD = 128
KV_RANK = 512
TOP = 6
BLOCK = 16
DEC_SLOTS = 4


ROPE_BASE = 50000.0
ROUTE_SCALE = 2.446
EPSILON = 1e-06
MASKED = -1e30


def rms_rows(values, scale_gain):
    values = values.astype(jnp.float32)
    inverse = lax.rsqrt(jnp.mean(values * values, axis=-1, keepdims=True) + EPSILON)
    return values * inverse * scale_gain


def angles(position, rope_width):
    half_width = rope_width // 2
    freq_steps = jnp.arange(half_width).astype(jnp.float32) * (2.0 / rope_width)
    frequency = jnp.exp(-math.log(ROPE_BASE) * freq_steps)
    return position.astype(jnp.float32)[:, None] * frequency[None, :]


def rotate(values, rot_angle):
    half_width = values.shape[-1] // 2
    first_half = values[..., :half_width].astype(jnp.float32)
    second_half = values[..., half_width:].astype(jnp.float32)
    cosine = jnp.cos(rot_angle)
    sine_part = jnp.sin(rot_angle)
    return jnp.concatenate(
        [
            first_half * cosine - second_half * sine_part,
            first_half * sine_part + second_half * cosine,
        ],
        axis=-1,
    )


def running(lengths):
    index = jnp.arange(lengths.shape[0])
    return jnp.sum(jnp.where(index[None, :] <= index[:, None], lengths[None, :], 0), axis=1)


def ranks(member):
    count = member.shape[-1]
    index = jnp.arange(count)
    before = (index[:, None] < index[None, :]).astype(jnp.bfloat16)
    return jnp.dot(member, before, preferred_element_type=jnp.float32).astype(jnp.int32)


def request_of(req_len, token_index):
    req_ends = running(req_len)
    return jnp.sum((token_index[:, None] >= req_ends[None, :]).astype(jnp.int32), axis=1)


def position_of(req_len, req_offset, token_index):
    request = request_of(req_len, token_index)
    req_ends = running(req_len)
    starts = req_ends - req_len
    member = request[:, None] == jnp.arange(req_len.shape[0])[None, :]
    start_at = jnp.sum(jnp.where(member, starts[None, :], 0), axis=1)
    offset = jnp.sum(jnp.where(member, req_offset[None, :], 0), axis=1)
    return offset + token_index - start_at


def key_width(piece_rows):
    for option_width in (1024, 512, 256, 128):
        return option_width
    return piece_rows


MESH = pl.DeviceIdType.MESH


def flip(place, step):
    return place + step * (1 - 2 * lax.rem(lax.div(place, step), 2))


def place_of(s, h, nz, back, turn):
    line = lax.rem(lax.div(s, 4) - back + nz, nz)
    block = line * 4 + lax.rem(s, 4)
    if turn & 1:
        block = flip(block, 2 - h)
    if turn & 2:
        block = flip(block, 1 + h)
    return block


def meet(s, h, nz):
    barrier = pltpu.get_barrier_semaphore()
    peers = [(place_of(s, h, nz, back, 0), h) for back in range(1, nz)]
    peers += [(flip(s, 2 - h), h), (flip(s, 1 + h), h), (s, 1 - h)]
    for peer in peers:
        pl.semaphore_signal(barrier, inc=1, device_id=peer, device_id_type=MESH)
    pl.semaphore_wait(barrier, len(peers))


class Spread:
    def __init__(self, buf, s, h, nz, sems):
        self.buf, self.s, self.h, self.nz = buf, s, h, nz
        self.sems = sems

    def move(self, block, kind, index, device):
        view = self.buf.at[self.h, block]
        return pltpu.make_async_remote_copy(
            src_ref=view,
            dst_ref=view,
            send_sem=self.sems[2 * kind].at[index],
            recv_sem=self.sems[2 * kind + 1].at[index],
            device_id=device,
            device_id_type=MESH,
        )

    def block(self, back, turn):
        return place_of(self.s, self.h, self.nz, back, turn)

    def line(self, ahead):
        device = (place_of(self.s, self.h, self.nz, self.nz - ahead, 0), self.h)
        return self.move(self.block(0, 0), 0, ahead, device)

    def line_in(self, back):
        return self.move(self.block(back, 0), 0, back, (self.s, 1 - self.h))

    def second(self, back, turn=0):
        return self.move(self.block(back, turn), 1, back, (flip(self.s, 2 - self.h), self.h))

    def third(self, back, side, turn=0):
        device = (flip(self.s, 1 + self.h), self.h)
        return self.move(self.block(back, turn + side), 2, 2 * back + side, device)

    def sibling(self, back, mine):
        half = self.h if mine else 1 - self.h
        line = lax.rem(lax.div(self.s, 4) - back + self.nz, self.nz)
        view = self.buf.at[half, pl.ds(line * 4, 4)]
        return pltpu.make_async_remote_copy(
            src_ref=view,
            dst_ref=view,
            send_sem=self.sems[6].at[back],
            recv_sem=self.sems[7].at[back],
            device_id=(self.s, 1 - self.h),
            device_id_type=MESH,
        )

    def send_all(self):
        for ahead in range(1, self.nz):
            self.line(ahead).start()
        for back in range(self.nz):
            if back:
                self.line_in(back).wait_recv()
            self.third(back, 0).start()
            self.second(back).start()
            self.second(back, 1).wait_recv()
            self.third(back, 1).start()

    def pass_on(self, back):
        for side in range(2):
            self.third(back, side, 2).wait_recv()
        self.sibling(back, True).start()

    def drain(self):
        for ahead in range(1, self.nz):
            self.line(ahead).wait_send()
        for back in range(self.nz):
            self.second(back).wait_send()
            self.third(back, 0).wait_send()
            self.third(back, 1).wait_send()
            self.sibling(back, True).wait_send()


def spread_sems(nz):
    dma = pltpu.SemaphoreType.DMA
    return [dma((nz,)), dma((nz,)), dma((nz,)), dma((nz,)), dma((2 * nz,)), dma((2 * nz,)), dma((nz,)), dma((nz,))]


def gather_kernel(nz, rows_ref, out_ref, *sems):
    s, h = lax.axis_index("seq"), lax.axis_index("head")
    half = rows_ref.shape[1]
    out_ref[h, s] = rows_ref[h]
    meet(s, h, nz)
    spread = Spread(out_ref, s, h, nz, sems)
    spread.send_all()
    for back in range(nz):
        spread.pass_on(back)
    for back in range(nz):
        spread.sibling(back, False).wait_recv()
    spread.drain()


def gather_rows(rows, seq_count):
    tok_rows, width = rows.shape
    nz = seq_count // 4
    out = pl.pallas_call(
        functools.partial(gather_kernel, nz),
        out_shape=jax.ShapeDtypeStruct((2, seq_count, tok_rows // 2, width), rows.dtype),
        in_specs=[pl.BlockSpec(memory_space=pltpu.VMEM)],
        out_specs=pl.BlockSpec(memory_space=pltpu.VMEM),
        scratch_shapes=spread_sems(nz),
        compiler_params=pltpu.CompilerParams(
            collective_id=0, has_side_effects=True, vmem_limit_bytes=16 * 1024 * 1024
        ),
    )(rows.reshape(2, tok_rows // 2, width))
    return jnp.swapaxes(out, 0, 1).reshape(seq_count * tok_rows, width)


def expert_kernel(
    nz,
    hidden_ref,
    attn_ref,
    gain_ref,
    pick_ref,
    place_ref,
    chosen_ref,
    router_ref,
    gate_up_hbm,
    down_hbm,
    out_ref,
    attn_in,
    mixed,
    x_buf,
    part,
    sib_buf,
    t3_buf,
    t2_buf,
    t1_buf,
    gate_up,
    down,
    rows_buf,
    act_buf,
    res_buf,
    load_sem,
    attn_sem,
    e0_send,
    e0_recv,
    e3_send,
    e3_recv,
    e2_send,
    e2_recv,
    e1_send,
    e1_recv,
    *sems,
):
    s, h = lax.axis_index("seq"), lax.axis_index("head")
    cols = hidden_ref.shape[1]
    half = cols // 2
    slots = pick_ref.shape[1]
    loads = [
        pltpu.make_async_copy(gate_up_hbm, gate_up, load_sem.at[0]),
        pltpu.make_async_copy(down_hbm, down, load_sem.at[1]),
    ]
    for load in loads:
        load.start()
    meet(s, h, nz)
    swap = pltpu.make_async_remote_copy(
        src_ref=attn_ref,
        dst_ref=attn_in,
        send_sem=attn_sem.at[0],
        recv_sem=attn_sem.at[1],
        device_id=(s, 1 - h),
        device_id_type=MESH,
    )
    swap.start()
    swap.wait_recv()
    total = hidden_ref[...].astype(jnp.float32) + (
        attn_ref[...].astype(jnp.float32) + attn_in[...].astype(jnp.float32)
    )
    mixed[0] = total[:, :half]
    mixed[1] = total[:, half:]
    inverse = lax.rsqrt(jnp.mean(total * total, axis=1, keepdims=True) + EPSILON)
    x_buf[h, s] = (mixed[h] * inverse * gain_ref[h][None, :]).astype(jnp.bfloat16)
    spread = Spread(x_buf, s, h, nz, sems)
    spread.send_all()
    spread.pass_on(0)
    for load in loads:
        load.wait()

    def remote(src, dst, send, recv, index, device):
        return pltpu.make_async_remote_copy(
            src_ref=src,
            dst_ref=dst,
            send_sem=send.at[index],
            recv_sem=recv.at[index],
            device_id=device,
            device_id_type=MESH,
        )

    sibling = (s, 1 - h)
    partner2 = (flip(s, 2 - h), h)
    partner3 = (flip(s, 1 + h), h)

    def line_of(back):
        return lax.rem(lax.div(s, 4) - back + nz, nz)

    def give0(back):
        base = pl.ds(line_of(back) * 4, 4)
        return remote(part.at[1 - h, base], sib_buf.at[base], e0_send, e0_recv, back, sibling)

    def give3(back, side):
        block = place_of(s, h, nz, back, 2 + side)
        index = 2 * back + side
        return remote(part.at[h, block], t3_buf.at[index], e3_send, e3_recv, index, partner3)

    def give2(back):
        block = place_of(s, h, nz, back, 1)
        return remote(part.at[h, block], t2_buf.at[back], e2_send, e2_recv, back, partner2)

    def give1(back):
        block = place_of(s, h, nz, back, 0)
        return remote(part.at[h, block], t1_buf.at[back], e1_send, e1_recv, back, (block, h))

    def add(block, other):
        part[h, block] = (
            part[h, block].astype(jnp.float32) + other.astype(jnp.float32)
        ).astype(jnp.bfloat16)

    def feed(back):
        spread.sibling(back, False).wait_recv()
        base = line_of(back) * 4
        for c in range(4):
            pick = pick_ref[base + c]
            for side in range(2):
                rows_buf[c * slots : (c + 1) * slots, side * half : (side + 1) * half] = jnp.dot(
                    pick, x_buf[side, base + c], preferred_element_type=jnp.float32
                ).astype(jnp.bfloat16)
        rows = rows_buf[...]
        logit = jnp.dot(rows, router_ref[...], preferred_element_type=jnp.float32)
        width = logit.shape[1] // 3
        logit = logit[:, :width] + (logit[:, width : 2 * width] + logit[:, 2 * width :])
        score = 1.0 / (1.0 + jnp.exp(-logit))
        chosen = score * chosen_ref[pl.ds(base, 4)].reshape(4 * slots, width)
        own = jnp.where(lax.broadcasted_iota(jnp.int32, chosen.shape, 1) == s, chosen, 0.0)
        own = jnp.sum(own, axis=1, keepdims=True)
        every = jnp.sum(chosen, axis=1, keepdims=True)
        weight = ROUTE_SCALE * own / jnp.where(every > 0.0, every, 1.0)
        gate = jnp.dot(rows, gate_up[0], preferred_element_type=jnp.float32)
        up = jnp.dot(rows, gate_up[1], preferred_element_type=jnp.float32)
        act_buf[...] = (gate / (1.0 + jnp.exp(-gate)) * up * weight).astype(jnp.bfloat16)
        res_buf[...] = jnp.dot(
            act_buf[...], down[...], preferred_element_type=jnp.float32
        ).astype(jnp.bfloat16)
        for c in range(4):
            for side in range(2):
                part[side, base + c] = jnp.dot(
                    place_ref[base + c],
                    res_buf[c * slots : (c + 1) * slots, side * half : (side + 1) * half],
                    preferred_element_type=jnp.float32,
                ).astype(jnp.bfloat16)
        give0(back).start()

    def fold0(back):
        give0(back).wait_recv()
        for turn in (2, 3, 1, 0):
            block = place_of(s, h, nz, back, turn)
            add(block, sib_buf[block])
            if turn >= 2:
                give3(back, turn - 2).start()

    def fold3(back):
        for side in (1, 0):
            give3(back, side).wait_recv()
            add(place_of(s, h, nz, back, side), t3_buf[2 * back + side])
            if side:
                give2(back).start()

    def fold2(back):
        give2(back).wait_recv()
        add(place_of(s, h, nz, back, 0), t2_buf[back])

        @pl.when(back > 0)
        def _():
            give1(back).start()

    @pl.loop(0, nz + 3)
    def _(step):
        @pl.when(step < nz)
        def _():
            feed(step)

        @pl.when(step < nz - 1)
        def _():
            spread.pass_on(step + 1)

        @pl.when((step >= 3))
        def _():
            fold2(step - 3)

        @pl.when((step >= 2) & (step < nz + 2))
        def _():
            fold3(step - 2)

        @pl.when((step >= 1) & (step < nz + 1))
        def _():
            fold0(step - 1)

    result = mixed[h] + part[h, s].astype(jnp.float32)
    for back in range(1, nz):
        give1(back).wait_recv()
        result = result + t1_buf[back].astype(jnp.float32)
    out_ref[...] = result.astype(out_ref.dtype)
    swap.wait_send()
    spread.drain()
    for back in range(nz):
        give0(back).wait_send()
        give3(back, 0).wait_send()
        give3(back, 1).wait_send()
        give2(back).wait_send()
        if back:
            give1(back).wait_send()


def expert_layer(hidden, attn_part, masks, ffn_gain, router, gate_up, down, seq_place, seq_count):
    tok_rows, cols = hidden.shape
    half = cols // 2
    nz = seq_count // 4
    expert_count = router.shape[1]
    hidden_units = down.shape[0]
    capacity = max(2, tok_rows * TOP * 4 // (3 * expert_count))
    mine = lax.dynamic_index_in_dim(masks, seq_place, 2, keepdims=False)
    rank = ranks(mine)
    slot = jnp.arange(capacity, dtype=jnp.int32)
    pick = (rank[:, None, :] == slot[None, :, None]) & (mine[:, None, :] > 0)
    pick = pick.astype(jnp.bfloat16)
    place = (rank[:, :, None] == slot[None, None, :]) & (mine[:, :, None] > 0)
    place = place.astype(jnp.bfloat16)
    wide_masks = jnp.pad(masks, ((0, 0), (0, 0), (0, 128 - expert_count)))
    chosen = jnp.einsum("brt,bte->bre", pick, wide_masks, preferred_element_type=jnp.float32)
    router = jnp.pad(router, ((0, 0), (0, 128 - expert_count)))
    high = lax.reduce_precision(router, 8, 7)
    middle = lax.reduce_precision(router - high, 8, 7)
    low = router - high - middle
    router3 = jnp.concatenate([high, middle, low], axis=1).astype(jnp.bfloat16)
    vmem = pl.BlockSpec(memory_space=pltpu.VMEM)
    hbm = pl.BlockSpec(memory_space=pl.ANY)
    dma = pltpu.SemaphoreType.DMA
    bf16 = jnp.bfloat16
    return pl.pallas_call(
        functools.partial(expert_kernel, nz),
        out_shape=jax.ShapeDtypeStruct((tok_rows, half), bf16),
        in_specs=[vmem] * 7 + [hbm] * 2,
        out_specs=vmem,
        scratch_shapes=[
            pltpu.VMEM((tok_rows, cols), bf16),
            pltpu.VMEM((2, tok_rows, half), jnp.float32),
            pltpu.VMEM((2, seq_count, tok_rows, half), bf16),
            pltpu.VMEM((2, seq_count, tok_rows, half), bf16),
            pltpu.VMEM((seq_count, tok_rows, half), bf16),
            pltpu.VMEM((2 * nz, tok_rows, half), bf16),
            pltpu.VMEM((nz, tok_rows, half), bf16),
            pltpu.VMEM((nz, tok_rows, half), bf16),
            pltpu.VMEM(gate_up.shape, bf16),
            pltpu.VMEM(down.shape, bf16),
            pltpu.VMEM((4 * capacity, cols), bf16),
            pltpu.VMEM((4 * capacity, hidden_units), bf16),
            pltpu.VMEM((4 * capacity, cols), bf16),
            dma((2,)),
            dma((2,)),
            dma((nz,)),
            dma((nz,)),
            dma((2 * nz,)),
            dma((2 * nz,)),
            dma((nz,)),
            dma((nz,)),
            dma((nz,)),
            dma((nz,)),
        ]
        + spread_sems(nz),
        compiler_params=pltpu.CompilerParams(
            collective_id=1, has_side_effects=True, vmem_limit_bytes=56 * 1024 * 1024
        ),
    )(hidden, attn_part, ffn_gain.reshape(2, half), pick, place, chosen, router3, gate_up, down)


def body(
    hidden,
    queries,
    req_len,
    req_offset,
    expert_ids,
    decode_slot,
    attn_gain,
    kv_down,
    kv_gain,
    key_up,
    value_up,
    out_proj,
    ffn_gain,
    router,
    expert_gate_up,
    expert_down,
):
    head_count = lax.axis_size("head")
    seq_place = lax.axis_index("seq")
    head_place = lax.axis_index("head")
    tok_rows = hidden.shape[0]
    heads_here = key_up.shape[0]
    my_index = seq_place * tok_rows + jnp.arange(tok_rows, dtype=jnp.int32)
    my_request = request_of(req_len, my_index)
    my_turn = angles(position_of(req_len, req_offset, my_index), ROPE)
    normed = rms_rows(hidden, attn_gain).astype(jnp.bfloat16)
    head_view = queries.reshape(tok_rows, heads_here, NOPE + ROPE)
    query_rope = rotate(head_view[:, :, NOPE:], my_turn[:, None, :]).astype(jnp.bfloat16)
    query_latent = jnp.einsum(
        "thn,hnc->thc", head_view[:, :, :NOPE], key_up, preferred_element_type=jnp.float32
    ).astype(jnp.bfloat16)
    query_rows = tok_rows * heads_here
    flat_latent = query_latent.reshape(query_rows, KV_RANK)
    flat_rope = query_rope.reshape(query_rows, ROPE)
    row_token = jnp.repeat(my_index, heads_here)
    row_request = jnp.repeat(my_request, heads_here)
    score_scale = 1.0 / math.sqrt(NOPE + ROPE)
    my_device = seq_place * head_count + head_place
    slot_ids = my_device * DEC_SLOTS + jnp.arange(DEC_SLOTS, dtype=jnp.int32)
    block_ids = jnp.arange(decode_slot.shape[0], dtype=jnp.int32)
    slot_match = decode_slot[None, :] == slot_ids[:, None]
    source_block = jnp.sum(jnp.where(slot_match, block_ids[None, :], 0), axis=1)
    slot_filled = jnp.any(slot_match, axis=1)
    kv_full = jnp.dot(normed, kv_down, preferred_element_type=jnp.float32)
    latent = rms_rows(kv_full[:, :KV_RANK], kv_gain).astype(jnp.bfloat16)
    key_rope = rotate(kv_full[:, KV_RANK:], my_turn).astype(jnp.bfloat16)
    run_peak = jnp.full((query_rows,), MASKED, jnp.float32)
    run_total = jnp.zeros((query_rows,), jnp.float32)
    run_acc = jnp.zeros((query_rows, KV_RANK), jnp.float32)
    expert_count = router.shape[1]
    expert_axis = jnp.arange(expert_count, dtype=jnp.int32)
    seq_count = lax.axis_size("seq")
    fast = seq_count % 4 == 0 and seq_count <= 16 and head_count == 2 and expert_count <= 64
    if fast:
        route_mask = jnp.any(expert_ids[:, :, None] == expert_axis[None, None, :], axis=1)
        payload = jnp.concatenate([latent, key_rope, route_mask.astype(jnp.bfloat16)], axis=1)
        payload = jnp.pad(payload, ((0, 0), (0, -payload.shape[1] % 128)))
        gathered = gather_rows(payload, seq_count)
        piece_latent = gathered[:, :KV_RANK]
        piece_rope = gathered[:, KV_RANK : KV_RANK + ROPE]
        all_masks = gathered[:, KV_RANK + ROPE : KV_RANK + ROPE + expert_count]
    else:
        piece_latent = lax.all_gather(latent, "seq", axis=0, tiled=True)
        piece_rope = lax.all_gather(key_rope, "seq", axis=0, tiled=True)
    piece_rows = piece_latent.shape[0]
    block_width = key_width(piece_rows)

    def key_block(block_no, loop_state):
        peak_now, total_now, acc_now = loop_state
        offset_rows = block_no * block_width
        block_latent = lax.dynamic_slice_in_dim(piece_latent, offset_rows, block_width, 0)
        block_rope = lax.dynamic_slice_in_dim(piece_rope, offset_rows, block_width, 0)
        key_index = offset_rows + jnp.arange(block_width, dtype=jnp.int32)
        key_request = request_of(req_len, key_index)
        contract = (((1,), (1,)), ((), ()))
        scores = lax.dot_general(
            flat_latent, block_latent, contract, preferred_element_type=jnp.float32
        )
        scores = (
            scores
            + lax.dot_general(flat_rope, block_rope, contract, preferred_element_type=jnp.float32)
        ) * score_scale
        allowed = (key_index[None, :] <= row_token[:, None]) & (
            key_request[None, :] == row_request[:, None]
        )
        scores = jnp.where(allowed, scores, MASKED)
        new_peak = jnp.maximum(peak_now, jnp.max(scores, axis=1))
        exp_terms = jnp.where(allowed, jnp.exp(scores - new_peak[:, None]), 0.0)
        fade_factor = jnp.exp(peak_now - new_peak)
        total_now = total_now * fade_factor + jnp.sum(exp_terms, axis=1)
        acc_now = acc_now * fade_factor[:, None] + jnp.dot(
            exp_terms.astype(jnp.bfloat16), block_latent, preferred_element_type=jnp.float32
        )
        return (new_peak, total_now, acc_now)

    run_peak, run_total, run_acc = lax.fori_loop(
        0, piece_rows // block_width, key_block, (run_peak, run_total, run_acc)
    )
    block_count = piece_rows // BLOCK
    pick_matrix = (
        source_block[:, None] == jnp.arange(block_count, dtype=jnp.int32)[None, :]
    ) & slot_filled[:, None]
    pick_matrix = pick_matrix.astype(jnp.bfloat16)
    slot_latent = jnp.dot(
        pick_matrix,
        piece_latent.reshape(block_count, BLOCK * KV_RANK),
        preferred_element_type=jnp.float32,
    )
    slot_rope = jnp.dot(
        pick_matrix,
        piece_rope.reshape(block_count, BLOCK * ROPE),
        preferred_element_type=jnp.float32,
    )
    folded = (run_peak, run_total, run_acc, slot_latent, slot_rope)
    run_total = folded[1]
    run_acc = folded[2]
    slot_latent = folded[3]
    slot_rope = folded[4]
    attended = (
        (run_acc / run_total[:, None]).astype(jnp.bfloat16).reshape(tok_rows, heads_here, KV_RANK)
    )
    head_out = jnp.einsum(
        "thc,hcv->thv", attended, value_up, preferred_element_type=jnp.float32
    ).astype(jnp.bfloat16)
    attn_part = jnp.dot(
        head_out.reshape(tok_rows, heads_here * V_HEAD),
        out_proj,
        preferred_element_type=jnp.float32,
    )
    decode_latent = slot_latent.astype(jnp.bfloat16).reshape(DEC_SLOTS, BLOCK, KV_RANK)
    decode_rope = slot_rope.astype(jnp.bfloat16)
    if fast:
        output = expert_layer(
            hidden,
            attn_part.astype(jnp.bfloat16),
            all_masks.reshape(seq_count, tok_rows, expert_count),
            ffn_gain,
            router,
            expert_gate_up[0],
            expert_down[0],
            seq_place,
            seq_count,
        )
        return (output, decode_latent, decode_rope)
    mixed_rows = hidden.astype(jnp.float32) + lax.psum(
        attn_part.astype(jnp.bfloat16), "head"
    ).astype(jnp.float32)
    moe_in = rms_rows(mixed_rows, ffn_gain).astype(jnp.bfloat16)
    capacity = max(2, tok_rows * TOP * 4 // (3 * expert_count))
    gate_score = jax.nn.sigmoid(
        jnp.dot(moe_in.astype(jnp.float32), router, precision=lax.Precision.HIGHEST)
    )
    id_match = expert_ids[:, :, None] == expert_axis[None, None, :]
    chosen = jnp.sum(jnp.where(id_match, gate_score[:, None, :], 0.0), axis=2)
    gate_weight = ROUTE_SCALE * chosen / jnp.sum(chosen, axis=1, keepdims=True)
    flat_ids = expert_ids.reshape(-1)
    one_hot = (flat_ids[:, None] == expert_axis[None, :]).astype(jnp.int32)
    earlier = ranks(one_hot.T.astype(jnp.bfloat16)).T
    slot_rank = jnp.sum(earlier * one_hot, axis=1)
    flat_slot = flat_ids * capacity + slot_rank
    owner_token = jnp.repeat(jnp.arange(tok_rows, dtype=jnp.int32), TOP)
    slot_token = jnp.zeros((expert_count * capacity,), jnp.int32).at[flat_slot].set(owner_token)
    slot_used = jnp.zeros((expert_count * capacity,), jnp.bool_).at[flat_slot].set(True)
    send_rows = jnp.where(
        slot_used[:, None], moe_in[slot_token], jnp.zeros((), jnp.bfloat16)
    ).reshape(expert_count, capacity, D)
    gate_up_local = expert_gate_up[0]
    down_local = expert_down[0]
    quarter_cols = D // head_count
    arrived = lax.all_to_all(send_rows, "seq", split_axis=0, concat_axis=0, tiled=True)
    sources, item_count, width_cols = arrived.shape
    flat_rows = arrived.reshape(sources * item_count, width_cols)
    gate_part = jnp.dot(flat_rows, gate_up_local[0], preferred_element_type=jnp.float32)
    up_part = jnp.dot(flat_rows, gate_up_local[1], preferred_element_type=jnp.float32)
    activated = (jax.nn.silu(gate_part) * up_part).astype(jnp.bfloat16)
    part_out = (
        jnp.dot(activated, down_local, preferred_element_type=jnp.float32)
        .astype(jnp.bfloat16)
        .reshape(sources, item_count, width_cols)
    )
    returned = lax.all_to_all(part_out, "seq", split_axis=0, concat_axis=0, tiled=True)
    back_cols = returned.shape[2]
    picked = returned.reshape(expert_count * capacity, back_cols)[flat_slot].reshape(
        tok_rows, TOP, back_cols
    )
    weighted = jnp.sum(picked.astype(jnp.float32) * gate_weight[:, :, None], axis=1)
    moe_out = lax.psum_scatter(
        weighted.astype(jnp.bfloat16), "head", scatter_dimension=1, tiled=True
    ).astype(jnp.float32)
    residual_part = lax.dynamic_slice_in_dim(mixed_rows, head_place * quarter_cols, quarter_cols, 1)
    output = (residual_part + moe_out).astype(jnp.bfloat16)
    return (output, decode_latent, decode_rope)


def solution(mesh):
    placed = (
        P("seq", None),
        P("seq", "head"),
        P(),
        P(),
        P("seq", None),
        P(),
        P(),
        P(),
        P(),
        P("head", None, None),
        P("head", None, None),
        P("head", None),
        P(),
        P(),
        P("seq", None, None, "head"),
        P("seq", "head", None),
    )
    return jax.shard_map(
        body,
        mesh=mesh,
        in_specs=placed,
        out_specs=(P("seq", "head"), P(("seq", "head"), None, None), P(("seq", "head"), None)),
        check_vma=False,
    )
```

```python
import functools
import math

import jax
import jax.numpy as jnp
from jax import lax
from jax.experimental import pallas as pl
from jax.experimental.pallas import tpu as pltpu
from jax.sharding import PartitionSpec as P

D = 2048
NOPE = 128
ROPE = 64
V_HEAD = 128
KV_RANK = 512
TOP = 6
BLOCK = 16
DEC_SLOTS = 4


ROPE_BASE = 50000.0
ROUTE_SCALE = 2.446
EPSILON = 1e-06
MASKED = -1e30


def rms_rows(values, scale_gain):
    values = values.astype(jnp.float32)
    inverse = lax.rsqrt(jnp.mean(values * values, axis=-1, keepdims=True) + EPSILON)
    return values * inverse * scale_gain


def angles(position, rope_width):
    half_width = rope_width // 2
    freq_steps = jnp.arange(half_width).astype(jnp.float32) * (2.0 / rope_width)
    frequency = jnp.exp(-math.log(ROPE_BASE) * freq_steps)
    return position.astype(jnp.float32)[:, None] * frequency[None, :]


def rotate(values, rot_angle):
    half_width = values.shape[-1] // 2
    first_half = values[..., :half_width].astype(jnp.float32)
    second_half = values[..., half_width:].astype(jnp.float32)
    cosine = jnp.cos(rot_angle)
    sine_part = jnp.sin(rot_angle)
    return jnp.concatenate(
        [
            first_half * cosine - second_half * sine_part,
            first_half * sine_part + second_half * cosine,
        ],
        axis=-1,
    )


def running(lengths):
    index = jnp.arange(lengths.shape[0])
    return jnp.sum(jnp.where(index[None, :] <= index[:, None], lengths[None, :], 0), axis=1)


def ranks(member):
    count = member.shape[-1]
    index = jnp.arange(count)
    before = (index[:, None] < index[None, :]).astype(jnp.bfloat16)
    return jnp.dot(member, before, preferred_element_type=jnp.float32).astype(jnp.int32)


def request_of(req_len, token_index):
    req_ends = running(req_len)
    return jnp.sum((token_index[:, None] >= req_ends[None, :]).astype(jnp.int32), axis=1)


def position_of(req_len, req_offset, token_index):
    request = request_of(req_len, token_index)
    req_ends = running(req_len)
    starts = req_ends - req_len
    member = request[:, None] == jnp.arange(req_len.shape[0])[None, :]
    start_at = jnp.sum(jnp.where(member, starts[None, :], 0), axis=1)
    offset = jnp.sum(jnp.where(member, req_offset[None, :], 0), axis=1)
    return offset + token_index - start_at


def key_width(piece_rows):
    for option_width in (1024, 512, 256, 128):
        return option_width
    return piece_rows


MESH = pl.DeviceIdType.MESH


def flip(place, step):
    return place + step * (1 - 2 * lax.rem(lax.div(place, step), 2))


def place_of(s, h, nz, back, turn):
    line = lax.rem(lax.div(s, 4) - back + nz, nz)
    block = line * 4 + lax.rem(s, 4)
    if turn & 1:
        block = flip(block, 2 - h)
    if turn & 2:
        block = flip(block, 1 + h)
    return block


def meet(s, h, nz):
    barrier = pltpu.get_barrier_semaphore()
    peers = [(place_of(s, h, nz, back, 0), h) for back in range(1, nz)]
    peers += [(flip(s, 2 - h), h), (flip(s, 1 + h), h), (s, 1 - h)]
    for peer in peers:
        pl.semaphore_signal(barrier, inc=1, device_id=peer, device_id_type=MESH)
    pl.semaphore_wait(barrier, len(peers))


class Spread:
    def __init__(self, buf, s, h, nz, sems, blocks_first=False):
        self.blocks_first = blocks_first
        self.buf, self.s, self.h, self.nz = buf, s, h, nz
        self.sems = sems

    def move(self, block, kind, index, device):
        view = self.buf.at[block, self.h] if self.blocks_first else self.buf.at[self.h, block]
        return pltpu.make_async_remote_copy(
            src_ref=view,
            dst_ref=view,
            send_sem=self.sems[2 * kind].at[index],
            recv_sem=self.sems[2 * kind + 1].at[index],
            device_id=device,
            device_id_type=MESH,
        )

    def block(self, back, turn):
        return place_of(self.s, self.h, self.nz, back, turn)

    def line(self, ahead):
        device = (place_of(self.s, self.h, self.nz, self.nz - ahead, 0), self.h)
        return self.move(self.block(0, 0), 0, ahead, device)

    def line_in(self, back):
        return self.move(self.block(back, 0), 0, back, (self.s, 1 - self.h))

    def second(self, back, turn=0):
        return self.move(self.block(back, turn), 1, back, (flip(self.s, 2 - self.h), self.h))

    def third(self, back, side, turn=0):
        device = (flip(self.s, 1 + self.h), self.h)
        return self.move(self.block(back, turn + side), 2, 2 * back + side, device)

    def sibling(self, back, mine):
        half = self.h if mine else 1 - self.h
        line = lax.rem(lax.div(self.s, 4) - back + self.nz, self.nz)
        four = pl.ds(line * 4, 4)
        view = self.buf.at[four, half] if self.blocks_first else self.buf.at[half, four]
        return pltpu.make_async_remote_copy(
            src_ref=view,
            dst_ref=view,
            send_sem=self.sems[6].at[back],
            recv_sem=self.sems[7].at[back],
            device_id=(self.s, 1 - self.h),
            device_id_type=MESH,
        )

    def send_all(self):
        for ahead in range(1, self.nz):
            self.line(ahead).start()
        for back in range(self.nz):
            if back:
                self.line_in(back).wait_recv()
            self.third(back, 0).start()
            self.second(back).start()
            self.second(back, 1).wait_recv()
            self.third(back, 1).start()

    def pass_on(self, back):
        for side in range(2):
            self.third(back, side, 2).wait_recv()
        self.sibling(back, True).start()

    def drain(self):
        for ahead in range(1, self.nz):
            self.line(ahead).wait_send()
        for back in range(self.nz):
            self.second(back).wait_send()
            self.third(back, 0).wait_send()
            self.third(back, 1).wait_send()
            self.sibling(back, True).wait_send()


def spread_sems(nz):
    dma = pltpu.SemaphoreType.DMA
    return [dma((nz,)), dma((nz,)), dma((nz,)), dma((nz,)), dma((2 * nz,)), dma((2 * nz,)), dma((nz,)), dma((nz,))]


def gather_kernel(nz, rows_ref, out_ref, *sems):
    s, h = lax.axis_index("seq"), lax.axis_index("head")
    out_ref[s, h] = rows_ref[h]
    meet(s, h, nz)
    spread = Spread(out_ref, s, h, nz, sems, True)
    spread.send_all()
    for back in range(nz):
        spread.pass_on(back)
    for back in range(nz):
        spread.sibling(back, False).wait_recv()
    spread.drain()


def gather_rows(rows, seq_count):
    tok_rows, width = rows.shape
    nz = seq_count // 4
    out = pl.pallas_call(
        functools.partial(gather_kernel, nz),
        out_shape=jax.ShapeDtypeStruct((seq_count, 2, tok_rows // 2, width), rows.dtype),
        in_specs=[pl.BlockSpec(memory_space=pltpu.VMEM)],
        out_specs=pl.BlockSpec(memory_space=pltpu.VMEM),
        scratch_shapes=spread_sems(nz),
        compiler_params=pltpu.CompilerParams(
            collective_id=0, has_side_effects=True, vmem_limit_bytes=16 * 1024 * 1024
        ),
    )(rows.reshape(2, tok_rows // 2, width))
    return out.reshape(seq_count * tok_rows, width)


def expert_kernel(
    nz,
    hidden_ref,
    attn_ref,
    gain_ref,
    pick_ref,
    place_ref,
    chosen_ref,
    router_ref,
    gate_up_hbm,
    down_hbm,
    out_ref,
    attn_in,
    mixed,
    x_buf,
    part,
    sib_buf,
    t3_buf,
    t2_buf,
    t1_buf,
    gate_up,
    down,
    rows_buf,
    act_buf,
    res_buf,
    load_sem,
    attn_sem,
    e0_send,
    e0_recv,
    e3_send,
    e3_recv,
    e2_send,
    e2_recv,
    e1_send,
    e1_recv,
    *sems,
):
    s, h = lax.axis_index("seq"), lax.axis_index("head")
    cols = hidden_ref.shape[1]
    half = cols // 2
    slots = pick_ref.shape[1]
    loads = [
        pltpu.make_async_copy(gate_up_hbm, gate_up, load_sem.at[0]),
        pltpu.make_async_copy(down_hbm, down, load_sem.at[1]),
    ]
    for load in loads:
        load.start()
    meet(s, h, nz)
    swap = pltpu.make_async_remote_copy(
        src_ref=attn_ref,
        dst_ref=attn_in,
        send_sem=attn_sem.at[0],
        recv_sem=attn_sem.at[1],
        device_id=(s, 1 - h),
        device_id_type=MESH,
    )
    swap.start()
    swap.wait_recv()
    total = hidden_ref[...].astype(jnp.float32) + (
        attn_ref[...].astype(jnp.float32) + attn_in[...].astype(jnp.float32)
    )
    mixed[0] = total[:, :half]
    mixed[1] = total[:, half:]
    inverse = lax.rsqrt(jnp.mean(total * total, axis=1, keepdims=True) + EPSILON)
    x_buf[h, s] = (mixed[h] * inverse * gain_ref[h][None, :]).astype(jnp.bfloat16)
    spread = Spread(x_buf, s, h, nz, sems)
    spread.send_all()
    spread.pass_on(0)
    for load in loads:
        load.wait()

    def remote(src, dst, send, recv, index, device):
        return pltpu.make_async_remote_copy(
            src_ref=src,
            dst_ref=dst,
            send_sem=send.at[index],
            recv_sem=recv.at[index],
            device_id=device,
            device_id_type=MESH,
        )

    sibling = (s, 1 - h)
    partner2 = (flip(s, 2 - h), h)
    partner3 = (flip(s, 1 + h), h)

    def line_of(back):
        return lax.rem(lax.div(s, 4) - back + nz, nz)

    def give0(back):
        base = pl.ds(line_of(back) * 4, 4)
        return remote(part.at[1 - h, base], sib_buf.at[base], e0_send, e0_recv, back, sibling)

    def give3(back, side):
        block = place_of(s, h, nz, back, 2 + side)
        index = 2 * back + side
        return remote(part.at[h, block], t3_buf.at[index], e3_send, e3_recv, index, partner3)

    def give2(back):
        block = place_of(s, h, nz, back, 1)
        return remote(part.at[h, block], t2_buf.at[back], e2_send, e2_recv, back, partner2)

    def give1(back):
        block = place_of(s, h, nz, back, 0)
        return remote(part.at[h, block], t1_buf.at[back], e1_send, e1_recv, back, (block, h))

    def add(block, other):
        part[h, block] = (
            part[h, block].astype(jnp.float32) + other.astype(jnp.float32)
        ).astype(jnp.bfloat16)

    def feed(back):
        spread.sibling(back, False).wait_recv()
        base = line_of(back) * 4
        for c in range(4):
            pick = pick_ref[base + c]
            for side in range(2):
                rows_buf[c * slots : (c + 1) * slots, side * half : (side + 1) * half] = jnp.dot(
                    pick, x_buf[side, base + c], preferred_element_type=jnp.float32
                ).astype(jnp.bfloat16)
        rows = rows_buf[...]
        logit = jnp.dot(rows, router_ref[...], preferred_element_type=jnp.float32)
        width = logit.shape[1] // 3
        logit = logit[:, :width] + (logit[:, width : 2 * width] + logit[:, 2 * width :])
        score = 1.0 / (1.0 + jnp.exp(-logit))
        chosen = score * chosen_ref[pl.ds(base, 4)].reshape(4 * slots, width)
        own = jnp.where(lax.broadcasted_iota(jnp.int32, chosen.shape, 1) == s, chosen, 0.0)
        own = jnp.sum(own, axis=1, keepdims=True)
        every = jnp.sum(chosen, axis=1, keepdims=True)
        weight = ROUTE_SCALE * own / jnp.where(every > 0.0, every, 1.0)
        across = (((1,), (1,)), ((), ()))
        gate = lax.dot_general(rows, gate_up[0], across, preferred_element_type=jnp.float32)
        up = lax.dot_general(rows, gate_up[1], across, preferred_element_type=jnp.float32)
        act_buf[...] = (gate / (1.0 + jnp.exp(-gate)) * up * weight).astype(jnp.bfloat16)
        res_buf[...] = jnp.dot(
            act_buf[...], down[...], preferred_element_type=jnp.float32
        ).astype(jnp.bfloat16)
        for c in range(4):
            for side in range(2):
                part[side, base + c] = jnp.dot(
                    place_ref[base + c],
                    res_buf[c * slots : (c + 1) * slots, side * half : (side + 1) * half],
                    preferred_element_type=jnp.float32,
                ).astype(jnp.bfloat16)
        give0(back).start()

    def fold0(back):
        give0(back).wait_recv()
        for turn in (2, 3, 1, 0):
            block = place_of(s, h, nz, back, turn)
            add(block, sib_buf[block])
            if turn >= 2:
                give3(back, turn - 2).start()

    def fold3(back):
        for side in (1, 0):
            give3(back, side).wait_recv()
            add(place_of(s, h, nz, back, side), t3_buf[2 * back + side])
            if side:
                give2(back).start()

    def fold2(back):
        give2(back).wait_recv()
        add(place_of(s, h, nz, back, 0), t2_buf[back])

        @pl.when(back > 0)
        def _():
            give1(back).start()

    @pl.loop(0, nz + 3)
    def _(step):
        @pl.when(step < nz)
        def _():
            feed(step)

        @pl.when(step < nz - 1)
        def _():
            spread.pass_on(step + 1)

        @pl.when((step >= 3))
        def _():
            fold2(step - 3)

        @pl.when((step >= 2) & (step < nz + 2))
        def _():
            fold3(step - 2)

        @pl.when((step >= 1) & (step < nz + 1))
        def _():
            fold0(step - 1)

    result = mixed[h] + part[h, s].astype(jnp.float32)
    for back in range(1, nz):
        give1(back).wait_recv()
        result = result + t1_buf[back].astype(jnp.float32)
    out_ref[...] = result.astype(out_ref.dtype)
    swap.wait_send()
    spread.drain()
    for back in range(nz):
        give0(back).wait_send()
        give3(back, 0).wait_send()
        give3(back, 1).wait_send()
        give2(back).wait_send()
        if back:
            give1(back).wait_send()


def expert_layer(hidden, attn_part, masks, ffn_gain, router, gate_up, down, seq_place, seq_count):
    tok_rows, cols = hidden.shape
    half = cols // 2
    nz = seq_count // 4
    expert_count = router.shape[1]
    hidden_units = down.shape[0]
    capacity = max(2, tok_rows * TOP * 4 // (3 * expert_count))
    mine = lax.dynamic_index_in_dim(masks, seq_place, 2, keepdims=False)
    rank = ranks(mine)
    slot = jnp.arange(capacity, dtype=jnp.int32)
    pick = (rank[:, None, :] == slot[None, :, None]) & (mine[:, None, :] > 0)
    pick = pick.astype(jnp.bfloat16)
    place = (rank[:, :, None] == slot[None, None, :]) & (mine[:, :, None] > 0)
    place = place.astype(jnp.bfloat16)
    wide_masks = jnp.pad(masks, ((0, 0), (0, 0), (0, 128 - expert_count)))
    chosen = jnp.einsum("brt,bte->bre", pick, wide_masks, preferred_element_type=jnp.float32)
    router = jnp.pad(router, ((0, 0), (0, 128 - expert_count)))
    high = lax.reduce_precision(router, 8, 7)
    middle = lax.reduce_precision(router - high, 8, 7)
    low = router - high - middle
    router3 = jnp.concatenate([high, middle, low], axis=1).astype(jnp.bfloat16)
    vmem = pl.BlockSpec(memory_space=pltpu.VMEM)
    hbm = pl.BlockSpec(memory_space=pl.ANY)
    dma = pltpu.SemaphoreType.DMA
    bf16 = jnp.bfloat16
    return pl.pallas_call(
        functools.partial(expert_kernel, nz),
        out_shape=jax.ShapeDtypeStruct((tok_rows, half), bf16),
        in_specs=[vmem] * 7 + [hbm] * 2,
        out_specs=vmem,
        scratch_shapes=[
            pltpu.VMEM((tok_rows, cols), bf16),
            pltpu.VMEM((2, tok_rows, half), jnp.float32),
            pltpu.VMEM((2, seq_count, tok_rows, half), bf16),
            pltpu.VMEM((2, seq_count, tok_rows, half), bf16),
            pltpu.VMEM((seq_count, tok_rows, half), bf16),
            pltpu.VMEM((2 * nz, tok_rows, half), bf16),
            pltpu.VMEM((nz, tok_rows, half), bf16),
            pltpu.VMEM((nz, tok_rows, half), bf16),
            pltpu.VMEM(gate_up.shape, bf16),
            pltpu.VMEM(down.shape, bf16),
            pltpu.VMEM((4 * capacity, cols), bf16),
            pltpu.VMEM((4 * capacity, hidden_units), bf16),
            pltpu.VMEM((4 * capacity, cols), bf16),
            dma((2,)),
            dma((2,)),
            dma((nz,)),
            dma((nz,)),
            dma((2 * nz,)),
            dma((2 * nz,)),
            dma((nz,)),
            dma((nz,)),
            dma((nz,)),
            dma((nz,)),
        ]
        + spread_sems(nz),
        compiler_params=pltpu.CompilerParams(
            collective_id=1, has_side_effects=True, vmem_limit_bytes=56 * 1024 * 1024
        ),
    )(hidden, attn_part, ffn_gain.reshape(2, half), pick, place, chosen, router3, gate_up, down)


def attend_kernel(
    key_tile,
    span_ref,
    first_ref,
    nope_ref,
    rope_ref,
    keys_ref,
    key_up_ref,
    value_up_ref,
    out_proj_ref,
    out_ref,
    query,
    acc,
    peak,
    total,
    heads_buf,
):
    heads, tok_rows = nope_ref.shape[0], nope_ref.shape[1]
    group = 4
    group_rows = group * tok_rows
    score_scale = 1.0 / math.sqrt(NOPE + ROPE)
    contract = (((1,), (1,)), ((), ()))
    for head in range(heads):
        here = slice(head * tok_rows, (head + 1) * tok_rows)
        query[here, :KV_RANK] = jnp.dot(
            nope_ref[head], key_up_ref[head], preferred_element_type=jnp.float32
        ).astype(jnp.bfloat16)
        query[here, KV_RANK:] = rope_ref[head]
    first = jnp.concatenate([first_ref[...]] * group, axis=0)
    own = span_ref[2] + lax.broadcasted_iota(jnp.int32, (tok_rows, 1), 0)
    own = jnp.concatenate([own] * group, axis=0)

    @pl.loop(0, heads // group)
    def _(part_no):
        base = pl.multiple_of(part_no * group_rows, group_rows)
        here = pl.ds(base, group_rows)
        peak[...] = jnp.full_like(peak, MASKED)
        total[...] = jnp.zeros_like(total)
        acc[...] = jnp.zeros_like(acc)

        @pl.loop(span_ref[0], span_ref[1])
        def _(tile):
            start = pl.multiple_of(tile * key_tile, key_tile)
            keys = keys_ref[pl.ds(start, key_tile), :]
            scores = score_scale * lax.dot_general(
                query[here, :], keys, contract, preferred_element_type=jnp.float32
            )
            index = start + lax.broadcasted_iota(jnp.int32, scores.shape, 1)
            allowed = (index <= own) & (index >= first)
            scores = jnp.where(allowed, scores, MASKED)
            old = peak[:, :1]
            new = jnp.maximum(old, jnp.max(scores, axis=1, keepdims=True))
            terms = jnp.where(allowed, jnp.exp(scores - new), 0.0)
            fade = jnp.exp(old - new)
            total[:, :1] = total[:, :1] * fade + jnp.sum(terms, axis=1, keepdims=True)
            peak[:, :1] = new
            acc[...] = acc[...] * fade + jnp.dot(
                terms.astype(jnp.bfloat16), keys[:, :KV_RANK], preferred_element_type=jnp.float32
            )

        attended = (acc[...] / total[:, :1]).astype(jnp.bfloat16)
        for member in range(group):
            heads_buf[part_no * group + member] = jnp.dot(
                attended[member * tok_rows : (member + 1) * tok_rows],
                value_up_ref[part_no * group + member],
                preferred_element_type=jnp.float32,
            ).astype(jnp.bfloat16)

    joined = jnp.concatenate([heads_buf[head] for head in range(heads)], axis=1)
    out_ref[...] = jnp.dot(
        joined, out_proj_ref[...], preferred_element_type=jnp.float32
    ).astype(out_ref.dtype)


def attend_rows(nope, rope, keys, key_up, value_up, out_proj, first, first_token):
    heads, tok_rows = nope.shape[0], nope.shape[1]
    key_tile = 512 if keys.shape[0] % 512 == 0 else 128
    width = keys.shape[1]
    span = jnp.stack(
        [
            jnp.min(first) // key_tile,
            (first_token + tok_rows + key_tile - 1) // key_tile,
            first_token,
        ]
    ).astype(jnp.int32)
    vmem = pl.BlockSpec(memory_space=pltpu.VMEM)
    rows = 4 * tok_rows
    return pl.pallas_call(
        functools.partial(attend_kernel, key_tile),
        out_shape=jax.ShapeDtypeStruct((tok_rows, out_proj.shape[1]), jnp.bfloat16),
        in_specs=[pl.BlockSpec(memory_space=pltpu.SMEM)] + [vmem] * 7,
        out_specs=vmem,
        scratch_shapes=[
            pltpu.VMEM((heads * tok_rows, width), jnp.bfloat16),
            pltpu.VMEM((rows, KV_RANK), jnp.float32),
            pltpu.VMEM((rows, 128), jnp.float32),
            pltpu.VMEM((rows, 128), jnp.float32),
            pltpu.VMEM((heads, tok_rows, V_HEAD), jnp.bfloat16),
        ],
        compiler_params=pltpu.CompilerParams(vmem_limit_bytes=40 * 1024 * 1024),
    )(span, first[:, None], nope, rope, keys, key_up, value_up, out_proj)


def body(
    hidden,
    queries,
    req_len,
    req_offset,
    expert_ids,
    decode_slot,
    attn_gain,
    kv_down,
    kv_gain,
    key_up,
    value_up,
    out_proj,
    ffn_gain,
    router,
    expert_gate_up,
    expert_down,
):
    head_count = lax.axis_size("head")
    seq_place = lax.axis_index("seq")
    head_place = lax.axis_index("head")
    tok_rows = hidden.shape[0]
    heads_here = key_up.shape[0]
    my_index = seq_place * tok_rows + jnp.arange(tok_rows, dtype=jnp.int32)
    my_request = request_of(req_len, my_index)
    my_turn = angles(position_of(req_len, req_offset, my_index), ROPE)
    normed = rms_rows(hidden, attn_gain).astype(jnp.bfloat16)
    head_view = queries.reshape(tok_rows, heads_here, NOPE + ROPE)
    query_rope = rotate(head_view[:, :, NOPE:], my_turn[:, None, :]).astype(jnp.bfloat16)
    query_latent = jnp.einsum(
        "thn,hnc->thc", head_view[:, :, :NOPE], key_up, preferred_element_type=jnp.float32
    ).astype(jnp.bfloat16)
    query_rows = tok_rows * heads_here
    flat_latent = query_latent.reshape(query_rows, KV_RANK)
    flat_rope = query_rope.reshape(query_rows, ROPE)
    row_token = jnp.repeat(my_index, heads_here)
    row_request = jnp.repeat(my_request, heads_here)
    score_scale = 1.0 / math.sqrt(NOPE + ROPE)
    my_device = seq_place * head_count + head_place
    slot_ids = my_device * DEC_SLOTS + jnp.arange(DEC_SLOTS, dtype=jnp.int32)
    block_ids = jnp.arange(decode_slot.shape[0], dtype=jnp.int32)
    slot_match = decode_slot[None, :] == slot_ids[:, None]
    source_block = jnp.sum(jnp.where(slot_match, block_ids[None, :], 0), axis=1)
    slot_filled = jnp.any(slot_match, axis=1)
    kv_full = jnp.dot(normed, kv_down, preferred_element_type=jnp.float32)
    latent = rms_rows(kv_full[:, :KV_RANK], kv_gain).astype(jnp.bfloat16)
    key_rope = rotate(kv_full[:, KV_RANK:], my_turn).astype(jnp.bfloat16)
    run_peak = jnp.full((query_rows,), MASKED, jnp.float32)
    run_total = jnp.zeros((query_rows,), jnp.float32)
    run_acc = jnp.zeros((query_rows, KV_RANK), jnp.float32)
    expert_count = router.shape[1]
    expert_axis = jnp.arange(expert_count, dtype=jnp.int32)
    seq_count = lax.axis_size("seq")
    fast = seq_count % 4 == 0 and seq_count <= 16 and head_count == 2 and expert_count <= 64
    if fast:
        route_mask = jnp.any(expert_ids[:, :, None] == expert_axis[None, None, :], axis=1)
        payload = jnp.concatenate([latent, key_rope, route_mask.astype(jnp.bfloat16)], axis=1)
        payload = jnp.pad(payload, ((0, 0), (0, -payload.shape[1] % 128)))
        gathered = gather_rows(payload, seq_count)
        all_masks = gathered[:, KV_RANK + ROPE : KV_RANK + ROPE + expert_count]
        by_head = jnp.swapaxes(head_view, 0, 1)
        rope_pad = gathered.shape[1] - KV_RANK - ROPE
        by_head_rope = jnp.pad(jnp.swapaxes(query_rope, 0, 1), ((0, 0), (0, 0), (0, rope_pad)))
        req_ends = running(req_len)
        member = my_request[:, None] == jnp.arange(req_len.shape[0])[None, :]
        first = jnp.sum(jnp.where(member, (req_ends - req_len)[None, :], 0), axis=1)
        attn_part = attend_rows(
            by_head[:, :, :NOPE],
            by_head_rope,
            gathered,
            key_up,
            value_up,
            out_proj,
            first,
            seq_place * tok_rows,
        )
        source_row = source_block[:, None] * BLOCK + jnp.arange(BLOCK, dtype=jnp.int32)[None, :]
        pick_rows = source_row[:, :, None] == jnp.arange(gathered.shape[0], dtype=jnp.int32)
        pick_rows = (pick_rows & slot_filled[:, None, None]).reshape(DEC_SLOTS * BLOCK, -1)
        slot_rows = jnp.dot(
            pick_rows.astype(jnp.bfloat16), gathered, preferred_element_type=jnp.float32
        ).astype(jnp.bfloat16)
        decode_latent = slot_rows[:, :KV_RANK].reshape(DEC_SLOTS, BLOCK, KV_RANK)
        decode_rope = slot_rows[:, KV_RANK : KV_RANK + ROPE].reshape(DEC_SLOTS, BLOCK * ROPE)
        output = expert_layer(
            hidden,
            attn_part,
            all_masks.reshape(seq_count, tok_rows, expert_count),
            ffn_gain,
            router,
            jnp.swapaxes(expert_gate_up[0], 1, 2),
            expert_down[0],
            seq_place,
            seq_count,
        )
        return (output, decode_latent, decode_rope)
    else:
        piece_latent = lax.all_gather(latent, "seq", axis=0, tiled=True)
        piece_rope = lax.all_gather(key_rope, "seq", axis=0, tiled=True)
    piece_rows = piece_latent.shape[0]
    block_width = key_width(piece_rows)

    def key_block(block_no, loop_state):
        peak_now, total_now, acc_now = loop_state
        offset_rows = block_no * block_width
        block_latent = lax.dynamic_slice_in_dim(piece_latent, offset_rows, block_width, 0)
        block_rope = lax.dynamic_slice_in_dim(piece_rope, offset_rows, block_width, 0)
        key_index = offset_rows + jnp.arange(block_width, dtype=jnp.int32)
        key_request = request_of(req_len, key_index)
        contract = (((1,), (1,)), ((), ()))
        scores = lax.dot_general(
            flat_latent, block_latent, contract, preferred_element_type=jnp.float32
        )
        scores = (
            scores
            + lax.dot_general(flat_rope, block_rope, contract, preferred_element_type=jnp.float32)
        ) * score_scale
        allowed = (key_index[None, :] <= row_token[:, None]) & (
            key_request[None, :] == row_request[:, None]
        )
        scores = jnp.where(allowed, scores, MASKED)
        new_peak = jnp.maximum(peak_now, jnp.max(scores, axis=1))
        exp_terms = jnp.where(allowed, jnp.exp(scores - new_peak[:, None]), 0.0)
        fade_factor = jnp.exp(peak_now - new_peak)
        total_now = total_now * fade_factor + jnp.sum(exp_terms, axis=1)
        acc_now = acc_now * fade_factor[:, None] + jnp.dot(
            exp_terms.astype(jnp.bfloat16), block_latent, preferred_element_type=jnp.float32
        )
        return (new_peak, total_now, acc_now)

    run_peak, run_total, run_acc = lax.fori_loop(
        0, piece_rows // block_width, key_block, (run_peak, run_total, run_acc)
    )
    block_count = piece_rows // BLOCK
    pick_matrix = (
        source_block[:, None] == jnp.arange(block_count, dtype=jnp.int32)[None, :]
    ) & slot_filled[:, None]
    pick_matrix = pick_matrix.astype(jnp.bfloat16)
    slot_latent = jnp.dot(
        pick_matrix,
        piece_latent.reshape(block_count, BLOCK * KV_RANK),
        preferred_element_type=jnp.float32,
    )
    slot_rope = jnp.dot(
        pick_matrix,
        piece_rope.reshape(block_count, BLOCK * ROPE),
        preferred_element_type=jnp.float32,
    )
    folded = (run_peak, run_total, run_acc, slot_latent, slot_rope)
    run_total = folded[1]
    run_acc = folded[2]
    slot_latent = folded[3]
    slot_rope = folded[4]
    attended = (
        (run_acc / run_total[:, None]).astype(jnp.bfloat16).reshape(tok_rows, heads_here, KV_RANK)
    )
    head_out = jnp.einsum(
        "thc,hcv->thv", attended, value_up, preferred_element_type=jnp.float32
    ).astype(jnp.bfloat16)
    attn_part = jnp.dot(
        head_out.reshape(tok_rows, heads_here * V_HEAD),
        out_proj,
        preferred_element_type=jnp.float32,
    )
    decode_latent = slot_latent.astype(jnp.bfloat16).reshape(DEC_SLOTS, BLOCK, KV_RANK)
    decode_rope = slot_rope.astype(jnp.bfloat16)
    mixed_rows = hidden.astype(jnp.float32) + lax.psum(
        attn_part.astype(jnp.bfloat16), "head"
    ).astype(jnp.float32)
    moe_in = rms_rows(mixed_rows, ffn_gain).astype(jnp.bfloat16)
    capacity = max(2, tok_rows * TOP * 4 // (3 * expert_count))
    gate_score = jax.nn.sigmoid(
        jnp.dot(moe_in.astype(jnp.float32), router, precision=lax.Precision.HIGHEST)
    )
    id_match = expert_ids[:, :, None] == expert_axis[None, None, :]
    chosen = jnp.sum(jnp.where(id_match, gate_score[:, None, :], 0.0), axis=2)
    gate_weight = ROUTE_SCALE * chosen / jnp.sum(chosen, axis=1, keepdims=True)
    flat_ids = expert_ids.reshape(-1)
    one_hot = (flat_ids[:, None] == expert_axis[None, :]).astype(jnp.int32)
    earlier = ranks(one_hot.T.astype(jnp.bfloat16)).T
    slot_rank = jnp.sum(earlier * one_hot, axis=1)
    flat_slot = flat_ids * capacity + slot_rank
    owner_token = jnp.repeat(jnp.arange(tok_rows, dtype=jnp.int32), TOP)
    slot_token = jnp.zeros((expert_count * capacity,), jnp.int32).at[flat_slot].set(owner_token)
    slot_used = jnp.zeros((expert_count * capacity,), jnp.bool_).at[flat_slot].set(True)
    send_rows = jnp.where(
        slot_used[:, None], moe_in[slot_token], jnp.zeros((), jnp.bfloat16)
    ).reshape(expert_count, capacity, D)
    gate_up_local = expert_gate_up[0]
    down_local = expert_down[0]
    quarter_cols = D // head_count
    arrived = lax.all_to_all(send_rows, "seq", split_axis=0, concat_axis=0, tiled=True)
    sources, item_count, width_cols = arrived.shape
    flat_rows = arrived.reshape(sources * item_count, width_cols)
    gate_part = jnp.dot(flat_rows, gate_up_local[0], preferred_element_type=jnp.float32)
    up_part = jnp.dot(flat_rows, gate_up_local[1], preferred_element_type=jnp.float32)
    activated = (jax.nn.silu(gate_part) * up_part).astype(jnp.bfloat16)
    part_out = (
        jnp.dot(activated, down_local, preferred_element_type=jnp.float32)
        .astype(jnp.bfloat16)
        .reshape(sources, item_count, width_cols)
    )
    returned = lax.all_to_all(part_out, "seq", split_axis=0, concat_axis=0, tiled=True)
    back_cols = returned.shape[2]
    picked = returned.reshape(expert_count * capacity, back_cols)[flat_slot].reshape(
        tok_rows, TOP, back_cols
    )
    weighted = jnp.sum(picked.astype(jnp.float32) * gate_weight[:, :, None], axis=1)
    moe_out = lax.psum_scatter(
        weighted.astype(jnp.bfloat16), "head", scatter_dimension=1, tiled=True
    ).astype(jnp.float32)
    residual_part = lax.dynamic_slice_in_dim(mixed_rows, head_place * quarter_cols, quarter_cols, 1)
    output = (residual_part + moe_out).astype(jnp.bfloat16)
    return (output, decode_latent, decode_rope)


def solution(mesh):
    placed = (
        P("seq", None),
        P("seq", "head"),
        P(),
        P(),
        P("seq", None),
        P(),
        P(),
        P(),
        P(),
        P("head", None, None),
        P("head", None, None),
        P("head", None),
        P(),
        P(),
        P("seq", None, None, "head"),
        P("seq", "head", None),
    )
    return jax.shard_map(
        body,
        mesh=mesh,
        in_specs=placed,
        out_specs=(P("seq", "head"), P(("seq", "head"), None, None), P(("seq", "head"), None)),
        check_vma=False,
    )
```

```python
import functools
import math

import jax
import jax.numpy as jnp
from jax import lax
from jax.experimental import pallas as pl
from jax.experimental.pallas import tpu as pltpu
from jax.sharding import PartitionSpec as P

D = 2048
NOPE = 128
ROPE = 64
V_HEAD = 128
KV_RANK = 512
TOP = 6
BLOCK = 16
DEC_SLOTS = 4


ROPE_BASE = 50000.0
ROUTE_SCALE = 2.446
EPSILON = 1e-06
MASKED = -1e30


def rms_rows(values, scale_gain):
    values = values.astype(jnp.float32)
    inverse = lax.rsqrt(jnp.mean(values * values, axis=-1, keepdims=True) + EPSILON)
    return values * inverse * scale_gain


def angles(position, rope_width):
    half_width = rope_width // 2
    freq_steps = jnp.arange(half_width).astype(jnp.float32) * (2.0 / rope_width)
    frequency = jnp.exp(-math.log(ROPE_BASE) * freq_steps)
    return position.astype(jnp.float32)[:, None] * frequency[None, :]


def rotate(values, rot_angle):
    half_width = values.shape[-1] // 2
    first_half = values[..., :half_width].astype(jnp.float32)
    second_half = values[..., half_width:].astype(jnp.float32)
    cosine = jnp.cos(rot_angle)
    sine_part = jnp.sin(rot_angle)
    return jnp.concatenate(
        [
            first_half * cosine - second_half * sine_part,
            first_half * sine_part + second_half * cosine,
        ],
        axis=-1,
    )


def running(lengths):
    index = jnp.arange(lengths.shape[0])
    return jnp.sum(jnp.where(index[None, :] <= index[:, None], lengths[None, :], 0), axis=1)


def ranks(member):
    count = member.shape[-1]
    index = jnp.arange(count)
    before = (index[:, None] < index[None, :]).astype(jnp.bfloat16)
    return jnp.dot(member, before, preferred_element_type=jnp.float32).astype(jnp.int32)


def request_of(req_len, token_index):
    req_ends = running(req_len)
    return jnp.sum((token_index[:, None] >= req_ends[None, :]).astype(jnp.int32), axis=1)


def position_of(req_len, req_offset, token_index):
    request = request_of(req_len, token_index)
    req_ends = running(req_len)
    starts = req_ends - req_len
    member = request[:, None] == jnp.arange(req_len.shape[0])[None, :]
    start_at = jnp.sum(jnp.where(member, starts[None, :], 0), axis=1)
    offset = jnp.sum(jnp.where(member, req_offset[None, :], 0), axis=1)
    return offset + token_index - start_at


def key_width(piece_rows):
    for option_width in (1024, 512, 256, 128):
        return option_width
    return piece_rows


MESH = pl.DeviceIdType.MESH


def flip(place, step):
    return place + step * (1 - 2 * lax.rem(lax.div(place, step), 2))


def place_of(s, h, nz, back, turn):
    line = lax.rem(lax.div(s, 4) - back + nz, nz)
    block = line * 4 + lax.rem(s, 4)
    if turn & 1:
        block = flip(block, 2 - h)
    if turn & 2:
        block = flip(block, 1 + h)
    return block


def meet(s, h, nz):
    barrier = pltpu.get_barrier_semaphore()
    peers = [(place_of(s, h, nz, back, 0), h) for back in range(1, nz)]
    peers += [(flip(s, 2 - h), h), (flip(s, 1 + h), h), (s, 1 - h)]
    for peer in peers:
        pl.semaphore_signal(barrier, inc=1, device_id=peer, device_id_type=MESH)
    pl.semaphore_wait(barrier, len(peers))


class Spread:
    def __init__(self, buf, s, h, nz, sems, blocks_first=False):
        self.blocks_first = blocks_first
        self.buf, self.s, self.h, self.nz = buf, s, h, nz
        self.sems = sems

    def move(self, block, kind, index, device):
        view = self.buf.at[block, self.h] if self.blocks_first else self.buf.at[self.h, block]
        return pltpu.make_async_remote_copy(
            src_ref=view,
            dst_ref=view,
            send_sem=self.sems[2 * kind].at[index],
            recv_sem=self.sems[2 * kind + 1].at[index],
            device_id=device,
            device_id_type=MESH,
        )

    def block(self, back, turn):
        return place_of(self.s, self.h, self.nz, back, turn)

    def line(self, ahead):
        device = (place_of(self.s, self.h, self.nz, self.nz - ahead, 0), self.h)
        return self.move(self.block(0, 0), 0, ahead, device)

    def line_in(self, back):
        return self.move(self.block(back, 0), 0, back, (self.s, 1 - self.h))

    def second(self, back, turn=0):
        return self.move(self.block(back, turn), 1, back, (flip(self.s, 2 - self.h), self.h))

    def third(self, back, side, turn=0):
        device = (flip(self.s, 1 + self.h), self.h)
        return self.move(self.block(back, turn + side), 2, 2 * back + side, device)

    def sibling(self, back, mine):
        half = self.h if mine else 1 - self.h
        line = lax.rem(lax.div(self.s, 4) - back + self.nz, self.nz)
        four = pl.ds(line * 4, 4)
        view = self.buf.at[four, half] if self.blocks_first else self.buf.at[half, four]
        return pltpu.make_async_remote_copy(
            src_ref=view,
            dst_ref=view,
            send_sem=self.sems[6].at[back],
            recv_sem=self.sems[7].at[back],
            device_id=(self.s, 1 - self.h),
            device_id_type=MESH,
        )

    def send_all(self):
        for ahead in range(1, self.nz):
            self.line(ahead).start()
        for back in range(self.nz):
            if back:
                self.line_in(back).wait_recv()
            self.third(back, 0).start()
            self.second(back).start()
            self.second(back, 1).wait_recv()
            self.third(back, 1).start()

    def pass_on(self, back):
        for side in range(2):
            self.third(back, side, 2).wait_recv()
        self.sibling(back, True).start()

    def drain(self):
        for ahead in range(1, self.nz):
            self.line(ahead).wait_send()
        for back in range(self.nz):
            self.second(back).wait_send()
            self.third(back, 0).wait_send()
            self.third(back, 1).wait_send()
            self.sibling(back, True).wait_send()


def spread_sems(nz):
    dma = pltpu.SemaphoreType.DMA
    return [dma((nz,)), dma((nz,)), dma((nz,)), dma((nz,)), dma((2 * nz,)), dma((2 * nz,)), dma((nz,)), dma((nz,))]


def gather_kernel(nz, rows_ref, out_ref, *sems):
    s, h = lax.axis_index("seq"), lax.axis_index("head")
    out_ref[s, h] = rows_ref[h]
    meet(s, h, nz)
    spread = Spread(out_ref, s, h, nz, sems, True)
    spread.send_all()
    for back in range(nz):
        spread.pass_on(back)
    for back in range(nz):
        spread.sibling(back, False).wait_recv()
    spread.drain()


def gather_rows(rows, seq_count):
    tok_rows, width = rows.shape
    nz = seq_count // 4
    out = pl.pallas_call(
        functools.partial(gather_kernel, nz),
        out_shape=jax.ShapeDtypeStruct((seq_count, 2, tok_rows // 2, width), rows.dtype),
        in_specs=[pl.BlockSpec(memory_space=pltpu.VMEM)],
        out_specs=pl.BlockSpec(memory_space=pltpu.VMEM),
        scratch_shapes=spread_sems(nz),
        compiler_params=pltpu.CompilerParams(
            collective_id=0, has_side_effects=True, vmem_limit_bytes=16 * 1024 * 1024
        ),
    )(rows.reshape(2, tok_rows // 2, width))
    return out.reshape(seq_count * tok_rows, width)


def expert_kernel(
    nz,
    hidden_ref,
    attn_ref,
    gain_ref,
    pick_ref,
    place_ref,
    chosen_ref,
    router_ref,
    gate_up_hbm,
    down_hbm,
    out_ref,
    attn_in,
    mixed,
    x_buf,
    part,
    sib_buf,
    t3_buf,
    t2_buf,
    t1_buf,
    gate_up,
    down,
    rows_buf,
    act_buf,
    res_buf,
    load_sem,
    attn_sem,
    e0_send,
    e0_recv,
    e3_send,
    e3_recv,
    e2_send,
    e2_recv,
    e1_send,
    e1_recv,
    *sems,
):
    s, h = lax.axis_index("seq"), lax.axis_index("head")
    cols = hidden_ref.shape[1]
    half = cols // 2
    slots = pick_ref.shape[1] // 2
    loads = [
        pltpu.make_async_copy(gate_up_hbm, gate_up, load_sem.at[0]),
        pltpu.make_async_copy(down_hbm, down, load_sem.at[1]),
    ]
    for load in loads:
        load.start()
    meet(s, h, nz)
    swap = pltpu.make_async_remote_copy(
        src_ref=attn_ref,
        dst_ref=attn_in,
        send_sem=attn_sem.at[0],
        recv_sem=attn_sem.at[1],
        device_id=(s, 1 - h),
        device_id_type=MESH,
    )
    swap.start()
    swap.wait_recv()
    total = hidden_ref[...].astype(jnp.float32) + (
        attn_ref[...].astype(jnp.float32) + attn_in[...].astype(jnp.float32)
    )
    mixed[0] = total[:, :half]
    mixed[1] = total[:, half:]
    inverse = lax.rsqrt(jnp.mean(total * total, axis=1, keepdims=True) + EPSILON)
    x_buf[h, s] = (mixed[h] * inverse * gain_ref[h][None, :]).astype(jnp.bfloat16)
    spread = Spread(x_buf, s, h, nz, sems)
    spread.send_all()
    spread.pass_on(0)
    for load in loads:
        load.wait()

    def remote(src, dst, send, recv, index, device):
        return pltpu.make_async_remote_copy(
            src_ref=src,
            dst_ref=dst,
            send_sem=send.at[index],
            recv_sem=recv.at[index],
            device_id=device,
            device_id_type=MESH,
        )

    sibling = (s, 1 - h)
    partner2 = (flip(s, 2 - h), h)
    partner3 = (flip(s, 1 + h), h)

    def line_of(back):
        return lax.rem(lax.div(s, 4) - back + nz, nz)

    def give0(back):
        base = pl.ds(line_of(back) * 4, 4)
        return remote(part.at[1 - h, base], sib_buf.at[base], e0_send, e0_recv, back, sibling)

    def give3(back, side):
        block = place_of(s, h, nz, back, 2 + side)
        index = 2 * back + side
        return remote(part.at[h, block], t3_buf.at[index], e3_send, e3_recv, index, partner3)

    def give2(back):
        block = place_of(s, h, nz, back, 1)
        return remote(part.at[h, block], t2_buf.at[back], e2_send, e2_recv, back, partner2)

    def give1(back):
        block = place_of(s, h, nz, back, 0)
        return remote(part.at[h, block], t1_buf.at[back], e1_send, e1_recv, back, (block, h))

    def add(block, other):
        part[h, block] = (
            part[h, block].astype(jnp.float32) + other.astype(jnp.float32)
        ).astype(jnp.bfloat16)

    def feed(back):
        spread.sibling(back, False).wait_recv()
        base = line_of(back) * 4
        for c in range(2):
            pick = pick_ref[line_of(back) * 2 + c]
            for side in range(2):
                pair = x_buf[side, pl.ds(base + 2 * c, 2)].reshape(pick.shape[1], half)
                rows_buf[2 * c * slots : 2 * (c + 1) * slots, side * half : (side + 1) * half] = (
                    jnp.dot(pick, pair, preferred_element_type=jnp.float32).astype(jnp.bfloat16)
                )
        rows = rows_buf[...]
        logit = jnp.dot(rows, router_ref[...], preferred_element_type=jnp.float32)
        width = logit.shape[1] // 3
        logit = logit[:, :width] + (logit[:, width : 2 * width] + logit[:, 2 * width :])
        score = 1.0 / (1.0 + jnp.exp(-logit))
        chosen = score * chosen_ref[pl.ds(base, 4)].reshape(4 * slots, width)
        own = jnp.where(lax.broadcasted_iota(jnp.int32, chosen.shape, 1) == s, chosen, 0.0)
        own = jnp.sum(own, axis=1, keepdims=True)
        every = jnp.sum(chosen, axis=1, keepdims=True)
        weight = ROUTE_SCALE * own / jnp.where(every > 0.0, every, 1.0)
        across = (((1,), (1,)), ((), ()))
        gate = lax.dot_general(rows, gate_up[0], across, preferred_element_type=jnp.float32)
        up = lax.dot_general(rows, gate_up[1], across, preferred_element_type=jnp.float32)
        act_buf[...] = (gate / (1.0 + jnp.exp(-gate)) * up * weight).astype(jnp.bfloat16)
        res_buf[...] = jnp.dot(
            act_buf[...], down[...], preferred_element_type=jnp.float32
        ).astype(jnp.bfloat16)
        for side in range(2):
            for c in range(2):
                pair = jnp.dot(
                    place_ref[line_of(back) * 2 + c],
                    res_buf[2 * c * slots : 2 * (c + 1) * slots, side * half : (side + 1) * half],
                    preferred_element_type=jnp.float32,
                ).astype(jnp.bfloat16)
                part[side, pl.ds(base + 2 * c, 2)] = pair.reshape(2, -1, half)
        give0(back).start()

    def fold0(back):
        give0(back).wait_recv()
        for turn in (2, 3, 1, 0):
            block = place_of(s, h, nz, back, turn)
            add(block, sib_buf[block])
            if turn >= 2:
                give3(back, turn - 2).start()

    def fold3(back):
        for side in (1, 0):
            give3(back, side).wait_recv()
            add(place_of(s, h, nz, back, side), t3_buf[2 * back + side])
            if side:
                give2(back).start()

    def fold2(back):
        give2(back).wait_recv()
        add(place_of(s, h, nz, back, 0), t2_buf[back])

        @pl.when(back > 0)
        def _():
            give1(back).start()

    @pl.loop(0, nz + 3)
    def _(step):
        @pl.when(step < nz)
        def _():
            feed(step)

        @pl.when(step < nz - 1)
        def _():
            spread.pass_on(step + 1)

        @pl.when((step >= 3))
        def _():
            fold2(step - 3)

        @pl.when((step >= 2) & (step < nz + 2))
        def _():
            fold3(step - 2)

        @pl.when((step >= 1) & (step < nz + 1))
        def _():
            fold0(step - 1)

    result = mixed[h] + part[h, s].astype(jnp.float32)
    for back in range(1, nz):
        give1(back).wait_recv()
        result = result + t1_buf[back].astype(jnp.float32)
    out_ref[...] = result.astype(out_ref.dtype)
    swap.wait_send()
    spread.drain()
    for back in range(nz):
        give0(back).wait_send()
        give3(back, 0).wait_send()
        give3(back, 1).wait_send()
        give2(back).wait_send()
        if back:
            give1(back).wait_send()


def paired(blocks):
    count, rows, cols = blocks.shape
    same = jnp.eye(2, dtype=blocks.dtype)[None, :, None, :, None]
    return (blocks.reshape(count // 2, 2, rows, 1, cols) * same).reshape(-1, 2 * rows, 2 * cols)


def expert_layer(hidden, attn_part, masks, ffn_gain, router, gate_up, down, seq_place, seq_count):
    tok_rows, cols = hidden.shape
    half = cols // 2
    nz = seq_count // 4
    expert_count = router.shape[1]
    hidden_units = down.shape[0]
    capacity = max(2, tok_rows * TOP * 4 // (3 * expert_count))
    mine = lax.dynamic_index_in_dim(masks, seq_place, 2, keepdims=False)
    rank = ranks(mine)
    slot = jnp.arange(capacity, dtype=jnp.int32)
    pick = (rank[:, None, :] == slot[None, :, None]) & (mine[:, None, :] > 0)
    pick = pick.astype(jnp.bfloat16)
    place = (rank[:, :, None] == slot[None, None, :]) & (mine[:, :, None] > 0)
    place = place.astype(jnp.bfloat16)
    wide_masks = jnp.pad(masks, ((0, 0), (0, 0), (0, 128 - expert_count)))
    chosen = jnp.einsum("brt,bte->bre", pick, wide_masks, preferred_element_type=jnp.float32)
    pick = paired(pick)
    place = paired(place)
    router = jnp.pad(router, ((0, 0), (0, 128 - expert_count)))
    high = lax.reduce_precision(router, 8, 7)
    middle = lax.reduce_precision(router - high, 8, 7)
    low = router - high - middle
    router3 = jnp.concatenate([high, middle, low], axis=1).astype(jnp.bfloat16)
    vmem = pl.BlockSpec(memory_space=pltpu.VMEM)
    hbm = pl.BlockSpec(memory_space=pl.ANY)
    dma = pltpu.SemaphoreType.DMA
    bf16 = jnp.bfloat16
    return pl.pallas_call(
        functools.partial(expert_kernel, nz),
        out_shape=jax.ShapeDtypeStruct((tok_rows, half), bf16),
        in_specs=[vmem] * 7 + [hbm] * 2,
        out_specs=vmem,
        scratch_shapes=[
            pltpu.VMEM((tok_rows, cols), bf16),
            pltpu.VMEM((2, tok_rows, half), jnp.float32),
            pltpu.VMEM((2, seq_count, tok_rows, half), bf16),
            pltpu.VMEM((2, seq_count, tok_rows, half), bf16),
            pltpu.VMEM((seq_count, tok_rows, half), bf16),
            pltpu.VMEM((2 * nz, tok_rows, half), bf16),
            pltpu.VMEM((nz, tok_rows, half), bf16),
            pltpu.VMEM((nz, tok_rows, half), bf16),
            pltpu.VMEM(gate_up.shape, bf16),
            pltpu.VMEM(down.shape, bf16),
            pltpu.VMEM((4 * capacity, cols), bf16),
            pltpu.VMEM((4 * capacity, hidden_units), bf16),
            pltpu.VMEM((4 * capacity, cols), bf16),
            dma((2,)),
            dma((2,)),
            dma((nz,)),
            dma((nz,)),
            dma((2 * nz,)),
            dma((2 * nz,)),
            dma((nz,)),
            dma((nz,)),
            dma((nz,)),
            dma((nz,)),
        ]
        + spread_sems(nz),
        compiler_params=pltpu.CompilerParams(
            collective_id=1, has_side_effects=True, vmem_limit_bytes=56 * 1024 * 1024
        ),
    )(hidden, attn_part, ffn_gain.reshape(2, half), pick, place, chosen, router3, gate_up, down)


def attend_kernel(
    key_tile,
    span_ref,
    first_ref,
    nope_ref,
    rope_ref,
    keys_ref,
    key_up_ref,
    value_up_ref,
    out_proj_ref,
    out_ref,
    query,
    acc,
    peak,
    total,
    heads_buf,
):
    heads, tok_rows = nope_ref.shape[0], nope_ref.shape[1]
    group = 4
    group_rows = group * tok_rows
    score_scale = 1.0 / math.sqrt(NOPE + ROPE)
    contract = (((1,), (1,)), ((), ()))
    for head in range(heads):
        here = slice(head * tok_rows, (head + 1) * tok_rows)
        query[here, :KV_RANK] = jnp.dot(
            nope_ref[head], key_up_ref[head], preferred_element_type=jnp.float32
        ).astype(jnp.bfloat16)
        query[here, KV_RANK:] = rope_ref[head]
    first = jnp.concatenate([first_ref[...]] * group, axis=0)
    own = span_ref[2] + lax.broadcasted_iota(jnp.int32, (tok_rows, 1), 0)
    own = jnp.concatenate([own] * group, axis=0)

    @pl.loop(0, heads // group)
    def _(part_no):
        base = pl.multiple_of(part_no * group_rows, group_rows)
        here = pl.ds(base, group_rows)
        peak[...] = jnp.full_like(peak, MASKED)
        total[...] = jnp.zeros_like(total)
        acc[...] = jnp.zeros_like(acc)

        @pl.loop(span_ref[0], span_ref[1])
        def _(tile):
            start = pl.multiple_of(tile * key_tile, key_tile)
            keys = keys_ref[pl.ds(start, key_tile), :]
            scores = score_scale * lax.dot_general(
                query[here, :], keys, contract, preferred_element_type=jnp.float32
            )
            index = start + lax.broadcasted_iota(jnp.int32, scores.shape, 1)
            allowed = (index <= own) & (index >= first)
            scores = jnp.where(allowed, scores, MASKED)
            old = peak[:, :1]
            new = jnp.maximum(old, jnp.max(scores, axis=1, keepdims=True))
            terms = jnp.where(allowed, jnp.exp(scores - new), 0.0)
            fade = jnp.exp(old - new)
            total[:, :1] = total[:, :1] * fade + jnp.sum(terms, axis=1, keepdims=True)
            peak[:, :1] = new
            acc[...] = acc[...] * fade + jnp.dot(
                terms.astype(jnp.bfloat16), keys[:, :KV_RANK], preferred_element_type=jnp.float32
            )

        attended = (acc[...] / total[:, :1]).astype(jnp.bfloat16)
        for member in range(group):
            heads_buf[part_no * group + member] = jnp.dot(
                attended[member * tok_rows : (member + 1) * tok_rows],
                value_up_ref[part_no * group + member],
                preferred_element_type=jnp.float32,
            ).astype(jnp.bfloat16)

    joined = jnp.concatenate([heads_buf[head] for head in range(heads)], axis=1)
    out_ref[...] = jnp.dot(
        joined, out_proj_ref[...], preferred_element_type=jnp.float32
    ).astype(out_ref.dtype)


def attend_rows(nope, rope, keys, key_up, value_up, out_proj, first, first_token):
    heads, tok_rows = nope.shape[0], nope.shape[1]
    key_tile = 512 if keys.shape[0] % 512 == 0 else 128
    width = keys.shape[1]
    span = jnp.stack(
        [
            jnp.min(first) // key_tile,
            (first_token + tok_rows + key_tile - 1) // key_tile,
            first_token,
        ]
    ).astype(jnp.int32)
    vmem = pl.BlockSpec(memory_space=pltpu.VMEM)
    rows = 4 * tok_rows
    return pl.pallas_call(
        functools.partial(attend_kernel, key_tile),
        out_shape=jax.ShapeDtypeStruct((tok_rows, out_proj.shape[1]), jnp.bfloat16),
        in_specs=[pl.BlockSpec(memory_space=pltpu.SMEM)] + [vmem] * 7,
        out_specs=vmem,
        scratch_shapes=[
            pltpu.VMEM((heads * tok_rows, width), jnp.bfloat16),
            pltpu.VMEM((rows, KV_RANK), jnp.float32),
            pltpu.VMEM((rows, 128), jnp.float32),
            pltpu.VMEM((rows, 128), jnp.float32),
            pltpu.VMEM((heads, tok_rows, V_HEAD), jnp.bfloat16),
        ],
        compiler_params=pltpu.CompilerParams(vmem_limit_bytes=40 * 1024 * 1024),
    )(span, first[:, None], nope, rope, keys, key_up, value_up, out_proj)


def body(
    hidden,
    queries,
    req_len,
    req_offset,
    expert_ids,
    decode_slot,
    attn_gain,
    kv_down,
    kv_gain,
    key_up,
    value_up,
    out_proj,
    ffn_gain,
    router,
    expert_gate_up,
    expert_down,
):
    head_count = lax.axis_size("head")
    seq_place = lax.axis_index("seq")
    head_place = lax.axis_index("head")
    tok_rows = hidden.shape[0]
    heads_here = key_up.shape[0]
    my_index = seq_place * tok_rows + jnp.arange(tok_rows, dtype=jnp.int32)
    my_request = request_of(req_len, my_index)
    my_turn = angles(position_of(req_len, req_offset, my_index), ROPE)
    normed = rms_rows(hidden, attn_gain).astype(jnp.bfloat16)
    head_view = queries.reshape(tok_rows, heads_here, NOPE + ROPE)
    query_rope = rotate(head_view[:, :, NOPE:], my_turn[:, None, :]).astype(jnp.bfloat16)
    query_latent = jnp.einsum(
        "thn,hnc->thc", head_view[:, :, :NOPE], key_up, preferred_element_type=jnp.float32
    ).astype(jnp.bfloat16)
    query_rows = tok_rows * heads_here
    flat_latent = query_latent.reshape(query_rows, KV_RANK)
    flat_rope = query_rope.reshape(query_rows, ROPE)
    row_token = jnp.repeat(my_index, heads_here)
    row_request = jnp.repeat(my_request, heads_here)
    score_scale = 1.0 / math.sqrt(NOPE + ROPE)
    my_device = seq_place * head_count + head_place
    slot_ids = my_device * DEC_SLOTS + jnp.arange(DEC_SLOTS, dtype=jnp.int32)
    block_ids = jnp.arange(decode_slot.shape[0], dtype=jnp.int32)
    slot_match = decode_slot[None, :] == slot_ids[:, None]
    source_block = jnp.sum(jnp.where(slot_match, block_ids[None, :], 0), axis=1)
    slot_filled = jnp.any(slot_match, axis=1)
    kv_full = jnp.dot(normed, kv_down, preferred_element_type=jnp.float32)
    latent = rms_rows(kv_full[:, :KV_RANK], kv_gain).astype(jnp.bfloat16)
    key_rope = rotate(kv_full[:, KV_RANK:], my_turn).astype(jnp.bfloat16)
    run_peak = jnp.full((query_rows,), MASKED, jnp.float32)
    run_total = jnp.zeros((query_rows,), jnp.float32)
    run_acc = jnp.zeros((query_rows, KV_RANK), jnp.float32)
    expert_count = router.shape[1]
    expert_axis = jnp.arange(expert_count, dtype=jnp.int32)
    seq_count = lax.axis_size("seq")
    fast = seq_count % 4 == 0 and seq_count <= 16 and head_count == 2 and expert_count <= 64
    if fast:
        route_mask = jnp.any(expert_ids[:, :, None] == expert_axis[None, None, :], axis=1)
        payload = jnp.concatenate([latent, key_rope, route_mask.astype(jnp.bfloat16)], axis=1)
        payload = jnp.pad(payload, ((0, 0), (0, -payload.shape[1] % 128)))
        gathered = gather_rows(payload, seq_count)
        all_masks = gathered[:, KV_RANK + ROPE : KV_RANK + ROPE + expert_count]
        by_head = jnp.swapaxes(head_view, 0, 1)
        rope_pad = gathered.shape[1] - KV_RANK - ROPE
        by_head_rope = jnp.pad(jnp.swapaxes(query_rope, 0, 1), ((0, 0), (0, 0), (0, rope_pad)))
        req_ends = running(req_len)
        member = my_request[:, None] == jnp.arange(req_len.shape[0])[None, :]
        first = jnp.sum(jnp.where(member, (req_ends - req_len)[None, :], 0), axis=1)
        attn_part = attend_rows(
            by_head[:, :, :NOPE],
            by_head_rope,
            gathered,
            key_up,
            value_up,
            out_proj,
            first,
            seq_place * tok_rows,
        )
        source_row = source_block[:, None] * BLOCK + jnp.arange(BLOCK, dtype=jnp.int32)[None, :]
        pick_rows = source_row[:, :, None] == jnp.arange(gathered.shape[0], dtype=jnp.int32)
        pick_rows = (pick_rows & slot_filled[:, None, None]).reshape(DEC_SLOTS * BLOCK, -1)
        slot_rows = jnp.dot(
            pick_rows.astype(jnp.bfloat16), gathered, preferred_element_type=jnp.float32
        ).astype(jnp.bfloat16)
        decode_latent = slot_rows[:, :KV_RANK].reshape(DEC_SLOTS, BLOCK, KV_RANK)
        decode_rope = slot_rows[:, KV_RANK : KV_RANK + ROPE].reshape(DEC_SLOTS, BLOCK * ROPE)
        output = expert_layer(
            hidden,
            attn_part,
            all_masks.reshape(seq_count, tok_rows, expert_count),
            ffn_gain,
            router,
            jnp.swapaxes(expert_gate_up[0], 1, 2),
            expert_down[0],
            seq_place,
            seq_count,
        )
        return (output, decode_latent, decode_rope)
    else:
        piece_latent = lax.all_gather(latent, "seq", axis=0, tiled=True)
        piece_rope = lax.all_gather(key_rope, "seq", axis=0, tiled=True)
    piece_rows = piece_latent.shape[0]
    block_width = key_width(piece_rows)

    def key_block(block_no, loop_state):
        peak_now, total_now, acc_now = loop_state
        offset_rows = block_no * block_width
        block_latent = lax.dynamic_slice_in_dim(piece_latent, offset_rows, block_width, 0)
        block_rope = lax.dynamic_slice_in_dim(piece_rope, offset_rows, block_width, 0)
        key_index = offset_rows + jnp.arange(block_width, dtype=jnp.int32)
        key_request = request_of(req_len, key_index)
        contract = (((1,), (1,)), ((), ()))
        scores = lax.dot_general(
            flat_latent, block_latent, contract, preferred_element_type=jnp.float32
        )
        scores = (
            scores
            + lax.dot_general(flat_rope, block_rope, contract, preferred_element_type=jnp.float32)
        ) * score_scale
        allowed = (key_index[None, :] <= row_token[:, None]) & (
            key_request[None, :] == row_request[:, None]
        )
        scores = jnp.where(allowed, scores, MASKED)
        new_peak = jnp.maximum(peak_now, jnp.max(scores, axis=1))
        exp_terms = jnp.where(allowed, jnp.exp(scores - new_peak[:, None]), 0.0)
        fade_factor = jnp.exp(peak_now - new_peak)
        total_now = total_now * fade_factor + jnp.sum(exp_terms, axis=1)
        acc_now = acc_now * fade_factor[:, None] + jnp.dot(
            exp_terms.astype(jnp.bfloat16), block_latent, preferred_element_type=jnp.float32
        )
        return (new_peak, total_now, acc_now)

    run_peak, run_total, run_acc = lax.fori_loop(
        0, piece_rows // block_width, key_block, (run_peak, run_total, run_acc)
    )
    block_count = piece_rows // BLOCK
    pick_matrix = (
        source_block[:, None] == jnp.arange(block_count, dtype=jnp.int32)[None, :]
    ) & slot_filled[:, None]
    pick_matrix = pick_matrix.astype(jnp.bfloat16)
    slot_latent = jnp.dot(
        pick_matrix,
        piece_latent.reshape(block_count, BLOCK * KV_RANK),
        preferred_element_type=jnp.float32,
    )
    slot_rope = jnp.dot(
        pick_matrix,
        piece_rope.reshape(block_count, BLOCK * ROPE),
        preferred_element_type=jnp.float32,
    )
    folded = (run_peak, run_total, run_acc, slot_latent, slot_rope)
    run_total = folded[1]
    run_acc = folded[2]
    slot_latent = folded[3]
    slot_rope = folded[4]
    attended = (
        (run_acc / run_total[:, None]).astype(jnp.bfloat16).reshape(tok_rows, heads_here, KV_RANK)
    )
    head_out = jnp.einsum(
        "thc,hcv->thv", attended, value_up, preferred_element_type=jnp.float32
    ).astype(jnp.bfloat16)
    attn_part = jnp.dot(
        head_out.reshape(tok_rows, heads_here * V_HEAD),
        out_proj,
        preferred_element_type=jnp.float32,
    )
    decode_latent = slot_latent.astype(jnp.bfloat16).reshape(DEC_SLOTS, BLOCK, KV_RANK)
    decode_rope = slot_rope.astype(jnp.bfloat16)
    mixed_rows = hidden.astype(jnp.float32) + lax.psum(
        attn_part.astype(jnp.bfloat16), "head"
    ).astype(jnp.float32)
    moe_in = rms_rows(mixed_rows, ffn_gain).astype(jnp.bfloat16)
    capacity = max(2, tok_rows * TOP * 4 // (3 * expert_count))
    gate_score = jax.nn.sigmoid(
        jnp.dot(moe_in.astype(jnp.float32), router, precision=lax.Precision.HIGHEST)
    )
    id_match = expert_ids[:, :, None] == expert_axis[None, None, :]
    chosen = jnp.sum(jnp.where(id_match, gate_score[:, None, :], 0.0), axis=2)
    gate_weight = ROUTE_SCALE * chosen / jnp.sum(chosen, axis=1, keepdims=True)
    flat_ids = expert_ids.reshape(-1)
    one_hot = (flat_ids[:, None] == expert_axis[None, :]).astype(jnp.int32)
    earlier = ranks(one_hot.T.astype(jnp.bfloat16)).T
    slot_rank = jnp.sum(earlier * one_hot, axis=1)
    flat_slot = flat_ids * capacity + slot_rank
    owner_token = jnp.repeat(jnp.arange(tok_rows, dtype=jnp.int32), TOP)
    slot_token = jnp.zeros((expert_count * capacity,), jnp.int32).at[flat_slot].set(owner_token)
    slot_used = jnp.zeros((expert_count * capacity,), jnp.bool_).at[flat_slot].set(True)
    send_rows = jnp.where(
        slot_used[:, None], moe_in[slot_token], jnp.zeros((), jnp.bfloat16)
    ).reshape(expert_count, capacity, D)
    gate_up_local = expert_gate_up[0]
    down_local = expert_down[0]
    quarter_cols = D // head_count
    arrived = lax.all_to_all(send_rows, "seq", split_axis=0, concat_axis=0, tiled=True)
    sources, item_count, width_cols = arrived.shape
    flat_rows = arrived.reshape(sources * item_count, width_cols)
    gate_part = jnp.dot(flat_rows, gate_up_local[0], preferred_element_type=jnp.float32)
    up_part = jnp.dot(flat_rows, gate_up_local[1], preferred_element_type=jnp.float32)
    activated = (jax.nn.silu(gate_part) * up_part).astype(jnp.bfloat16)
    part_out = (
        jnp.dot(activated, down_local, preferred_element_type=jnp.float32)
        .astype(jnp.bfloat16)
        .reshape(sources, item_count, width_cols)
    )
    returned = lax.all_to_all(part_out, "seq", split_axis=0, concat_axis=0, tiled=True)
    back_cols = returned.shape[2]
    picked = returned.reshape(expert_count * capacity, back_cols)[flat_slot].reshape(
        tok_rows, TOP, back_cols
    )
    weighted = jnp.sum(picked.astype(jnp.float32) * gate_weight[:, :, None], axis=1)
    moe_out = lax.psum_scatter(
        weighted.astype(jnp.bfloat16), "head", scatter_dimension=1, tiled=True
    ).astype(jnp.float32)
    residual_part = lax.dynamic_slice_in_dim(mixed_rows, head_place * quarter_cols, quarter_cols, 1)
    output = (residual_part + moe_out).astype(jnp.bfloat16)
    return (output, decode_latent, decode_rope)


def solution(mesh):
    placed = (
        P("seq", None),
        P("seq", "head"),
        P(),
        P(),
        P("seq", None),
        P(),
        P(),
        P(),
        P(),
        P("head", None, None),
        P("head", None, None),
        P("head", None),
        P(),
        P(),
        P("seq", None, None, "head"),
        P("seq", "head", None),
    )
    return jax.shard_map(
        body,
        mesh=mesh,
        in_specs=placed,
        out_specs=(P("seq", "head"), P(("seq", "head"), None, None), P(("seq", "head"), None)),
        check_vma=False,
    )
```
